256 devices in a mesh: ctx: 32 (over z, y_lo, core), grp: 8 (over y_hi, x).
Axes of the slice: x: 4, y: 4 (y_hi: 2, y_lo: 2; y = y_hi * 2 + y_lo), z: 8, core: 2. Of those that a mesh axis runs over, the one named last changes fastest.
Arguments:
- queries: bfloat16 [16384, 4096], P('ctx', 'grp'), may hold values from -6 to 6
- key_rows: bfloat16 [16384, 1024], P('ctx', 'grp'), may hold values from -6 to 6
- value_rows: bfloat16 [16384, 1024], P('ctx', 'grp'), may hold values from -6 to 6
- output_rows: bfloat16 [16384, 4096], P('ctx', 'grp'), may hold values from -6 to 6
- output_grad: bfloat16 [16384, 4096], P('ctx', 'grp'), may hold values from -6 to 6
- log_normalizer: float32 [16384, 32], P('ctx', 'grp'), may hold values from 4 to 6
- selection: int32 [32, 3], replicated, may hold values from 0 to 30, as said below
- query_weight: bfloat16 [4096, 4096], P(None, 'grp'), may hold values from -0.09375 to 0.09375
- key_weight: bfloat16 [4096, 1024], P(None, 'grp'), may hold values from -0.09375 to 0.09375
- value_weight: bfloat16 [4096, 1024], P(None, 'grp'), may hold values from -0.09375 to 0.09375
Outputs:
- input_grad: bfloat16 [16384, 4096], P('ctx', 'grp')
The draws below stay inside these ranges and needn't reach their ends.
Inputs may be any that keep to these rules, and one draw needn't show every extreme that they name: `selection`: row b names the 3 blocks chosen for query block b: distinct blocks below b, among them always block b - 1; a row with fewer than 3 blocks below it names all of them and repeats b itself in the remaining places.
All inputs are finite; a program needn't handle non-finite values.
Results may differ from the reference program's by a relative error of at most 0.019.
Values may be sent and summed in bfloat16 or wider, within the bound.
No kernel may reach another device: no remote copies, remote signals or barrier semaphores. Data moves between devices by JAX's collectives and lax.ppermute only.
A program may use at most 128 MiB of HBM per device.

```python
import jax
import jax.numpy as jnp
from jax import lax

D = 4096
HD = 128
QPK = 4
KV_DEV = 1
BLOCK = 512
TOPK = 3
KV_HEADS = 8
HEADS = 32
HF = 4096
KF = 1024
SEQ = 16384
NB = 32
N_GRP = 8


def draw_selection(key, part):
    key = jax.random.fold_in(key, 7)
    block_ids = jnp.arange(NB, dtype=jnp.int32)
    ranks = jax.random.randint(key, (NB, NB), 0, 1 << 20, dtype=jnp.int32) * NB + block_ids[None, :]
    ranks = jnp.where(block_ids[None, :] == block_ids[:, None] - 1, 1 << 30, ranks)
    ranks = jnp.where(block_ids[None, :] < block_ids[:, None], ranks, -1)
    values, indices = lax.top_k(ranks, TOPK)
    return jnp.where(values >= 0, indices, block_ids[:, None]).astype(jnp.int32)


def block_levels(own_key, shape, pieces, low, top_value):
    gain, own = 1.0, jax.random.fold_in(own_key, 6)
    for dim, blocks in pieces:
        steps = jnp.exp(jax.random.uniform(jax.random.fold_in(own, dim), (blocks,), jnp.float32, low / len(pieces), top_value / len(pieces)))
        gain = gain * jnp.repeat(steps, shape[dim] // blocks).reshape([-1 if axis == dim else 1 for axis in range(len(shape))])
    return gain


def gaussian(stream_key, extent, width, reach, pieces=(), held_as=jnp.bfloat16):
    entries = jax.random.normal(stream_key, extent, jnp.float32) * width
    if len(pieces) > 0:
        entries = block_levels(stream_key, extent, pieces, -0.22, 0.18) * entries
    return jnp.clip(entries, min=-reach, max=reach).astype(held_as)


def setup_inputs(seed: int = 0) -> dict:
    keys = jax.random.split(jax.random.key(seed), 11)
    queries = gaussian(keys[0], (SEQ, HF), 1.0, 6.0, ((0, 32), (1, 8)))
    key_rows = gaussian(keys[1], (SEQ, KF), 1.0, 6.0, ((0, 32), (1, 8)))
    value_rows = gaussian(keys[2], (SEQ, KF), 1.0, 6.0, ((0, 32), (1, 8)))
    output_rows = gaussian(keys[3], (SEQ, HF), 1.0, 6.0, ((0, 32), (1, 8)))
    output_grad = gaussian(keys[4], (SEQ, HF), 1.0, 6.0, ((0, 32), (1, 8)))
    log_normalizer = jnp.clip(4.0 + 2.0 * jax.random.uniform(keys[5], (SEQ, HEADS), jnp.float32) ** block_levels(keys[5], (SEQ, HEADS), ((0, 32), (1, 8)), -0.2, 0.2), 4.0, 6.0)
    selection = draw_selection(jax.random.fold_in(keys[10], 71), 0)
    query_weight = gaussian(keys[7], (D, HF), D ** -0.5, 0.09375, ((1, 8),))
    key_weight = gaussian(keys[8], (D, KF), D ** -0.5, 0.09375, ((1, 8),))
    value_weight = gaussian(keys[9], (D, KF), D ** -0.5, 0.09375, ((1, 8),))
    return dict(queries=queries, key_rows=key_rows, value_rows=value_rows, output_rows=output_rows, output_grad=output_grad, log_normalizer=log_normalizer, selection=selection, query_weight=query_weight, key_weight=key_weight, value_weight=value_weight)


def reference(queries, key_rows, value_rows, output_rows, output_grad, log_normalizer, selection, query_weight, key_weight, value_weight):
    scaling = float(HD) ** -0.5
    query_full = queries.astype(jnp.float32).reshape(SEQ, KV_HEADS, QPK, HD)
    key_full = key_rows.astype(jnp.float32).reshape(SEQ, KV_HEADS, HD)
    value_full = value_rows.astype(jnp.float32).reshape(SEQ, KV_HEADS, HD)
    output_full = output_rows.astype(jnp.float32).reshape(SEQ, KV_HEADS, QPK, HD)
    cotangent = output_grad.astype(jnp.float32).reshape(SEQ, KV_HEADS, QPK, HD)
    row_delta = jnp.sum(output_full * cotangent, axis=-1)
    norm_full = log_normalizer.reshape(SEQ, KV_HEADS, QPK)
    offsets = jnp.arange(BLOCK, dtype=jnp.int32)
    causal = offsets[None, :] <= offsets[:, None]

    def block_step(totals, block_index):
        key_total, value_total = totals
        row_start = block_index * BLOCK
        query_block = lax.dynamic_slice_in_dim(query_full, row_start, BLOCK, 0)
        grad_block = lax.dynamic_slice_in_dim(cotangent, row_start, BLOCK, 0)
        norm_block = lax.dynamic_slice_in_dim(norm_full, row_start, BLOCK, 0).transpose(1, 2, 0)[:, :, :, None]
        delta_block = lax.dynamic_slice_in_dim(row_delta, row_start, BLOCK, 0).transpose(1, 2, 0)[:, :, :, None]
        chosen_row = lax.dynamic_index_in_dim(selection, block_index, 0, keepdims=False).astype(jnp.int32)
        visited = jnp.concatenate([jnp.reshape(block_index, (1,)).astype(jnp.int32), chosen_row])
        keys_seen = jnp.concatenate([lax.dynamic_slice_in_dim(key_full, visited[column] * BLOCK, BLOCK, 0) for column in range(TOPK + 1)], axis=0)
        values_seen = jnp.concatenate([lax.dynamic_slice_in_dim(value_full, visited[column] * BLOCK, BLOCK, 0) for column in range(TOPK + 1)], axis=0)
        allowed = jnp.concatenate([causal] + [jnp.broadcast_to(visited[column] < block_index, (BLOCK, BLOCK)) for column in range(1, TOPK + 1)], axis=1)
        scores = jnp.einsum("qgpd,kgd->gpqk", query_block, keys_seen) * scaling
        probs = jnp.where(allowed[None, None], jnp.exp(scores - norm_block), 0.0)
        prob_grad = jnp.einsum("qgpd,kgd->gpqk", grad_block, values_seen)
        score_grad = probs * (prob_grad - delta_block)
        probs_half = lax.optimization_barrier(probs.astype(jnp.bfloat16)).astype(jnp.float32)
        score_half = lax.optimization_barrier(score_grad.astype(jnp.bfloat16)).astype(jnp.float32)
        value_part = jnp.einsum("gpqk,qgpd->kgd", probs_half, grad_block)
        key_part = jnp.einsum("gpqk,qgpd->kgd", score_half, query_block)
        query_grad = (jnp.einsum("gpqk,kgd->qgpd", score_half, keys_seen) * scaling).astype(jnp.bfloat16)
        for column in range(TOPK + 1):
            target = visited[column] * BLOCK
            key_total = lax.dynamic_update_slice_in_dim(key_total, lax.dynamic_slice_in_dim(key_total, target, BLOCK, 0) + key_part[column * BLOCK:(column + 1) * BLOCK], target, 0)
            value_total = lax.dynamic_update_slice_in_dim(value_total, lax.dynamic_slice_in_dim(value_total, target, BLOCK, 0) + value_part[column * BLOCK:(column + 1) * BLOCK], target, 0)
        return (key_total, value_total), query_grad

    zeroed = jnp.zeros((SEQ, KV_HEADS, HD), jnp.float32)
    (key_total, value_total), query_blocks = lax.scan(block_step, (zeroed, zeroed), jnp.arange(NB, dtype=jnp.int32))
    grad_query = query_blocks.reshape(SEQ, HEADS * HD)
    grad_key = (key_total * scaling).astype(jnp.bfloat16).reshape(SEQ, KV_HEADS * HD)
    grad_value = value_total.astype(jnp.bfloat16).reshape(SEQ, KV_HEADS * HD)
    query_width = QPK * KV_DEV * HD
    key_width = KV_DEV * HD
    combined = jnp.zeros((SEQ, D), jnp.float32)
    for group in range(N_GRP):
        query_cols = slice(group * query_width, (group + 1) * query_width)
        key_cols = slice(group * key_width, (group + 1) * key_width)
        partial_sum = jnp.dot(grad_query[:, query_cols], query_weight[:, query_cols].T, preferred_element_type=jnp.float32)
        partial_sum = partial_sum + jnp.dot(grad_key[:, key_cols], key_weight[:, key_cols].T, preferred_element_type=jnp.float32)
        partial_sum = partial_sum + jnp.dot(grad_value[:, key_cols], value_weight[:, key_cols].T, preferred_element_type=jnp.float32)
        combined = combined + lax.optimization_barrier(partial_sum.astype(jnp.bfloat16)).astype(jnp.float32)
    return combined.astype(jnp.bfloat16)
```

```python
import functools

import jax
import jax.numpy as jnp
from jax import lax
from jax.experimental import pallas as pl
from jax.experimental.pallas import tpu as pltpu
from jax.sharding import PartitionSpec as P

HD = 128
HEADS = 4
BLOCK = 512
BLOCKS = 32
PIECE = BLOCK // BLOCKS
SLOTS = 2
GROUPS = 8
SCALE = float(HD) ** (-0.5)
LOG2E = 1.4426950408889634
BF = jnp.bfloat16
F32 = jnp.float32
VMEM_BYTES = 50 * 1024 * 1024

PORTS = {"a": 1, "b": 3, "y": 4}
CHUNKS = ((0, 176, "aby"), (176, 176, "bya"), (352, 160, "yab"))

NT = (((1,), (1,)), ((), ()))


def others(selection, block):
    before = block - 1
    first, second, third = selection[block, 0], selection[block, 1], selection[block, 2]
    return jnp.where(first == before, second, first), jnp.where(third == before, second, third)


def pick_kernel(selection, pieces, out):
    def step(block, carry):
        for slot, chosen in enumerate(others(selection, block)):
            out[block, slot] = pieces[chosen]
        return carry

    lax.fori_loop(0, BLOCKS, step, 0)


def collect_kernel(selection, parts, out, total):
    total[...] = jnp.zeros_like(total)

    def step(block, carry):
        for slot, chosen in enumerate(others(selection, block)):

            @pl.when(chosen < block)
            def _():
                total[chosen] += parts[block, slot].astype(F32)

        return carry

    lax.fori_loop(0, BLOCKS, step, 0)
    out[...] = total[...].astype(BF)


def attention_kernel(
    place, selection, queries, output_grad, output_rows, norm, own, before, chosen,
    query_out, own_out, before_out, chosen_out,
    keys, values, keys_t, delta, query_total, key_total, value_total,
):
    block = place[0]
    picks = others(selection, block)
    norm_rows = norm[...] * LOG2E
    for head in range(HEADS):
        cols = pl.ds(head * HD, HD)
        product = output_rows[:, cols].astype(F32) * output_grad[:, cols].astype(F32)
        delta[head] = jnp.sum(product.T, axis=0, keepdims=True)
    query_total[...] = jnp.zeros_like(query_total)

    def tile(tile_norm, causal):
        key_total[...] = jnp.zeros_like(key_total)
        value_total[...] = jnp.zeros_like(value_total)
        key, value, key_t = keys[...], values[...], keys_t[...]

        def head_step(head, carry):
            cols = pl.ds(pl.multiple_of(head * HD, HD), HD)
            query, grad = queries[:, cols], output_grad[:, cols]
            scores = lax.dot_general(key, query, NT, preferred_element_type=F32)
            prob_grad = lax.dot_general(value, grad, NT, preferred_element_type=F32)
            probs = jnp.exp2(scores * (SCALE * LOG2E) - tile_norm[head] * LOG2E)
            if causal:
                shape = (BLOCK, BLOCK)
                seen = lax.broadcasted_iota(jnp.int32, shape, 0) <= lax.broadcasted_iota(jnp.int32, shape, 1)
                probs = jnp.where(seen, probs, 0.0)
            score_half = (probs * (prob_grad - delta[head])).astype(BF)
            value_total[...] += jnp.dot(probs.astype(BF), grad, preferred_element_type=F32)
            key_total[...] += jnp.dot(score_half, query, preferred_element_type=F32)
            query_total[head] += jnp.dot(key_t, score_half, preferred_element_type=F32)
            return carry

        lax.fori_loop(0, HEADS, head_step, 0)

    def load(key, value):
        keys[...] = key
        values[...] = value
        keys_t[...] = key.astype(F32).T.astype(BF)

    load(own[:, :HD], own[:, HD:])
    tile(norm, True)
    own_out[:, :HD] = key_total[...]
    own_out[:, HD:] = value_total[...]

    @pl.when(block > 0)
    def _():
        load(before[:, :HD], before[:, HD:])
        tile(norm, False)
        before_out[:, :HD] = key_total[...].astype(BF)
        before_out[:, HD:] = value_total[...].astype(BF)

    @pl.when(block == 0)
    def _():
        before_out[...] = jnp.zeros_like(before_out)

    for slot in range(SLOTS):

        @pl.when(picks[slot] < block)
        def _():
            load(
                chosen[:, slot, :, :HD].reshape(BLOCK, HD),
                chosen[:, slot, :, HD:].reshape(BLOCK, HD),
            )
            tile(norm, False)
            chosen_out[:, slot, :, :HD] = key_total[...].reshape(BLOCKS, PIECE, HD).astype(BF)
            chosen_out[:, slot, :, HD:] = value_total[...].reshape(BLOCKS, PIECE, HD).astype(BF)

        @pl.when(picks[slot] >= block)
        def _():
            chosen_out[:, slot] = jnp.zeros((BLOCKS, PIECE, 2 * HD), BF)

    for head in range(HEADS):
        query_out[:, head * HD : (head + 1) * HD] = (query_total[head].T * SCALE).astype(BF)


def project_kernel(place, query_grad, own, before, chosen, query_weight, key_weight, value_weight, *refs):
    outs, (key_grad, value_grad) = refs[: len(CHUNKS)], refs[len(CHUNKS) :]

    @pl.when(pl.program_id(0) == 0)
    def _():
        total = own[...] + before[...].astype(F32) + chosen[...].reshape(BLOCK, 2 * HD).astype(F32)
        key_grad[...] = (total[:, :HD] * SCALE).astype(BF)
        value_grad[...] = total[:, HD:].astype(BF)

    part = lax.dot_general(query_grad[...], query_weight[...], NT, preferred_element_type=F32)
    part += lax.dot_general(key_grad[...], key_weight[...], NT, preferred_element_type=F32)
    part += lax.dot_general(value_grad[...], value_weight[...], NT, preferred_element_type=F32)
    part = part.astype(BF)
    for (start, rows, _), out in zip(CHUNKS, outs):
        out[0] = part[start : start + rows]


def chunk_index(step, order):
    bits = {"a": step // 4, "b": step // 2 % 2, "y": step % 2}
    return bits[order[0]] * 4 + bits[order[1]] * 2 + bits[order[2]]


def weight_index(step, place):
    target = (step // 4) * PORTS["a"] ^ (step // 2 % 2) * PORTS["b"] ^ (step % 2) * PORTS["y"]
    return (place[0] ^ target, 0)


def project(place, query_grad, own, before, chosen, query_weight, key_weight, value_weight):
    model = query_weight.shape[0] // GROUPS
    whole = lambda array: pl.BlockSpec(array.shape, lambda step, place: (0,) * array.ndim)
    weight = lambda array: pl.BlockSpec((model, array.shape[1]), weight_index)
    return pl.pallas_call(
        project_kernel,
        grid_spec=pltpu.PrefetchScalarGridSpec(
            num_scalar_prefetch=1,
            grid=(GROUPS,),
            in_specs=[
                whole(query_grad), whole(own), whole(before), whole(chosen),
                weight(query_weight), weight(key_weight), weight(value_weight),
            ],
            out_specs=[
                pl.BlockSpec((1, rows, model), lambda step, place, order=order: (chunk_index(step, order), 0, 0))
                for _, rows, order in CHUNKS
            ],
            scratch_shapes=[pltpu.VMEM((BLOCK, HD), BF), pltpu.VMEM((BLOCK, HD), BF)],
        ),
        out_shape=[jax.ShapeDtypeStruct((GROUPS, rows, model), BF) for _, rows, _ in CHUNKS],
        compiler_params=pltpu.CompilerParams(vmem_limit_bytes=VMEM_BYTES),
    )(place, query_grad, own, before, chosen, query_weight, key_weight, value_weight)


def swap(value, port):
    return lax.ppermute(value, "grp", [(source, source ^ PORTS[port]) for source in range(GROUPS)])


def reduce_over_groups(parts):
    parts = list(parts)
    for stage in range(3):
        half = parts[0].shape[0] // 2
        sent = lax.optimization_barrier([part[half:] for part in parts])
        got = [swap(part, order[stage]) for part, (_, _, order) in zip(sent, CHUNKS)]
        got = lax.optimization_barrier(got)
        parts = [part[:half].astype(F32) + other.astype(F32) for part, other in zip(parts, got)]
        parts = [part.astype(BF) for part in parts]
    return jnp.concatenate([part[0] for part in parts], axis=0)


def on_device(
    queries, key_rows, value_rows, output_rows, output_grad, log_normalizer, selection,
    query_weight, key_weight, value_weight,
):
    smem = pl.BlockSpec(memory_space=pltpu.SMEM)
    vmem = pl.BlockSpec(memory_space=pltpu.VMEM)
    params = pltpu.CompilerParams(vmem_limit_bytes=VMEM_BYTES)
    place = lax.axis_index("ctx").astype(jnp.int32).reshape(1)
    group = lax.axis_index("grp").astype(jnp.int32).reshape(1)
    count = lax.axis_size("ctx")
    own = jnp.concatenate([key_rows, value_rows], axis=1)
    norm = log_normalizer.T.reshape(HEADS, 1, BLOCK)

    before = lax.ppermute(own, "ctx", [(i, (i + 1) % count) for i in range(count)])
    pieces = lax.all_to_all(own.reshape(BLOCKS, PIECE, 2 * HD), "ctx", 0, 0)
    picked = pl.pallas_call(
        pick_kernel,
        in_specs=[smem, vmem],
        out_specs=vmem,
        out_shape=jax.ShapeDtypeStruct((BLOCKS, SLOTS, PIECE, 2 * HD), BF),
        compiler_params=params,
    )(selection, pieces)
    chosen = lax.all_to_all(picked, "ctx", 0, 0)

    query_grad, own_grad, before_grad, chosen_grad = pl.pallas_call(
        attention_kernel,
        in_specs=[smem, smem] + [vmem] * 7,
        out_specs=[vmem] * 4,
        out_shape=[
            jax.ShapeDtypeStruct((BLOCK, HEADS * HD), BF),
            jax.ShapeDtypeStruct((BLOCK, 2 * HD), F32),
            jax.ShapeDtypeStruct((BLOCK, 2 * HD), BF),
            jax.ShapeDtypeStruct((BLOCKS, SLOTS, PIECE, 2 * HD), BF),
        ],
        scratch_shapes=[
            pltpu.VMEM((BLOCK, HD), BF),
            pltpu.VMEM((BLOCK, HD), BF),
            pltpu.VMEM((HD, BLOCK), BF),
            pltpu.VMEM((HEADS, 1, BLOCK), F32),
            pltpu.VMEM((HEADS, HD, BLOCK), F32),
            pltpu.VMEM((BLOCK, HD), F32),
            pltpu.VMEM((BLOCK, HD), F32),
        ],
        compiler_params=params,
    )(place, selection, queries, output_grad, output_rows, norm, own, before, chosen)

    before_sum = lax.ppermute(before_grad, "ctx", [(i, (i - 1) % count) for i in range(count)])
    returned = lax.all_to_all(chosen_grad, "ctx", 0, 0)
    collected = pl.pallas_call(
        collect_kernel,
        in_specs=[smem, vmem],
        out_specs=vmem,
        out_shape=jax.ShapeDtypeStruct((BLOCKS, PIECE, 2 * HD), BF),
        scratch_shapes=[pltpu.VMEM((BLOCKS, PIECE, 2 * HD), F32)],
        compiler_params=params,
    )(selection, returned)
    chosen_sum = lax.all_to_all(collected, "ctx", 0, 0)
    parts = project(
        group, query_grad, own_grad, before_sum, chosen_sum, query_weight, key_weight, value_weight
    )
    return reduce_over_groups(parts)


def solution(mesh):
    tokens = P("ctx", "grp")
    return jax.shard_map(
        on_device,
        mesh=mesh,
        in_specs=(tokens,) * 6 + (P(),) + (P(None, "grp"),) * 3,
        out_specs=tokens,
        check_vma=False,
    )
```

```python
import jax
import jax.numpy as jnp
from jax import lax
from jax.experimental import pallas as pl
from jax.experimental.pallas import tpu as pltpu
from jax.sharding import PartitionSpec as P

HD = 128
HEADS = 4
BLOCK = 512
BLOCKS = 32
PIECE = BLOCK // BLOCKS
SLOTS = 2
GROUPS = 8
SCALE = float(HD) ** (-0.5)
LOG2E = 1.4426950408889634
BF = jnp.bfloat16
F32 = jnp.float32
MIB = 1024 * 1024

PARTNERS = 3
HALVES = 2
OTHER = 4

NT = (((1,), (1,)), ((), ()))


def others(selection, block):
    before = block - 1
    first, second, third = selection[block, 0], selection[block, 1], selection[block, 2]
    return jnp.where(first == before, second, first), jnp.where(third == before, second, third)


def pick_kernel(selection, pieces, *refs):
    out = refs[-1]

    def step(block, carry):
        for slot, chosen in enumerate(others(selection, block)):
            out[block, slot] = pieces[chosen]
        return carry

    lax.fori_loop(0, BLOCKS, step, 0)


def collect_kernel(selection, parts, *refs):
    out, total = refs[-2:]
    total[...] = jnp.zeros_like(total)

    def step(block, carry):
        for slot, chosen in enumerate(others(selection, block)):

            @pl.when(chosen < block)
            def _():
                total[chosen] += parts[block, slot].astype(F32)

        return carry

    lax.fori_loop(0, BLOCKS, step, 0)
    out[...] = total[...].astype(BF)


def attend(queries, output_grad, norm, delta, scratch, causal):
    keys, values, keys_t, query_total, key_total, value_total = scratch
    key_total[...] = jnp.zeros_like(key_total)
    value_total[...] = jnp.zeros_like(value_total)
    key, value, key_t = keys[...], values[...], keys_t[...]

    def head_step(head, carry):
        cols = pl.ds(pl.multiple_of(head * HD, HD), HD)
        query, grad = queries[:, cols], output_grad[:, cols]
        scores = lax.dot_general(key, query, NT, preferred_element_type=F32)
        prob_grad = lax.dot_general(value, grad, NT, preferred_element_type=F32)
        probs = jnp.exp2(scores * (SCALE * LOG2E) - norm[head] * LOG2E)
        if causal:
            shape = (BLOCK, BLOCK)
            seen = lax.broadcasted_iota(jnp.int32, shape, 0) <= lax.broadcasted_iota(jnp.int32, shape, 1)
            probs = jnp.where(seen, probs, 0.0)
        score_half = (probs * (prob_grad - delta[head])).astype(BF)
        value_total[...] += jnp.dot(probs.astype(BF), grad, preferred_element_type=F32)
        key_total[...] += jnp.dot(score_half, query, preferred_element_type=F32)
        query_total[head] += jnp.dot(key_t, score_half, preferred_element_type=F32)
        return carry

    lax.fori_loop(0, HEADS, head_step, 0, unroll=True)


def load(scratch, key, value):
    keys, values, keys_t = scratch[:3]
    keys[...] = key
    values[...] = value
    keys_t[...] = key.astype(F32).T.astype(BF)


def near_kernel(
    place, queries, output_grad, output_rows, norm, own, before,
    delta, query_total, own_out, before_out, keys, values, keys_t, key_total, value_total,
):
    scratch = (keys, values, keys_t, query_total, key_total, value_total)
    for head in range(HEADS):
        cols = pl.ds(head * HD, HD)
        product = output_rows[:, cols].astype(F32) * output_grad[:, cols].astype(F32)
        delta[head] = jnp.sum(product.T, axis=0, keepdims=True)
    query_total[...] = jnp.zeros_like(query_total)
    load(scratch, own[:, :HD], own[:, HD:])
    attend(queries, output_grad, norm, delta, scratch, True)
    own_out[:, :HD] = key_total[...]
    own_out[:, HD:] = value_total[...]

    @pl.when(place[0] > 0)
    def _():
        load(scratch, before[:, :HD], before[:, HD:])
        attend(queries, output_grad, norm, delta, scratch, False)
        before_out[:, :HD] = key_total[...].astype(BF)
        before_out[:, HD:] = value_total[...].astype(BF)

    @pl.when(place[0] == 0)
    def _():
        before_out[...] = jnp.zeros_like(before_out)


def far_kernel(
    place, selection, queries, output_grad, norm, delta, query_near, chosen,
    query_out, chosen_out, keys, values, keys_t, query_total, key_total, value_total,
):
    scratch = (keys, values, keys_t, query_total, key_total, value_total)
    block = place[0]
    query_total[...] = query_near[...]
    for slot, pick in enumerate(others(selection, block)):

        @pl.when(pick < block)
        def _():
            load(
                scratch,
                chosen[:, slot, :, :HD].reshape(BLOCK, HD),
                chosen[:, slot, :, HD:].reshape(BLOCK, HD),
            )
            attend(queries, output_grad, norm, delta, scratch, False)
            chosen_out[:, slot, :, :HD] = key_total[...].reshape(BLOCKS, PIECE, HD).astype(BF)
            chosen_out[:, slot, :, HD:] = value_total[...].reshape(BLOCKS, PIECE, HD).astype(BF)

        @pl.when(pick >= block)
        def _():
            chosen_out[:, slot] = jnp.zeros((BLOCKS, PIECE, 2 * HD), BF)

    for head in range(HEADS):
        query_out[:, head * HD : (head + 1) * HD] = (query_total[head].T * SCALE).astype(BF)


def tile_scratch(with_query):
    shapes = [((BLOCK, HD), BF), ((BLOCK, HD), BF), ((HD, BLOCK), BF)]
    shapes += [((HEADS, HD, BLOCK), F32)] * with_query + [((BLOCK, HD), F32)] * 2
    return [pltpu.VMEM(shape, dtype) for shape, dtype in shapes]


def join_kernel(key_rows, value_rows, out):
    out[:, :HD] = key_rows[...]
    out[:, HD:] = value_rows[...]


def pack_kernel(place, query_weight, key_weight, value_weight, out):
    wide = HEADS * HD
    out[:, :wide] = query_weight[...]
    out[:, wide : wide + HD] = key_weight[...]
    out[:, wide + HD :] = value_weight[...]


def pack_weights(place, partner, *weights):
    rows = lambda step, place: (place[0] ^ (place[1] * OTHER) ^ partner, 0)
    shape = (BLOCK, (HEADS + 2) * HD)
    return pl.pallas_call(
        pack_kernel,
        grid_spec=pltpu.PrefetchScalarGridSpec(
            num_scalar_prefetch=1,
            grid=(1,),
            in_specs=[pl.BlockSpec((BLOCK, weight.shape[1]), rows) for weight in weights],
            out_specs=pl.BlockSpec(shape, lambda step, place: (0, 0)),
        ),
        out_shape=jax.ShapeDtypeStruct(shape, BF),
        cost_estimate=cost(0, 4 * shape[0] * shape[1]),
        compiler_params=pltpu.CompilerParams(vmem_limit_bytes=8 * MIB),
    )(place, *weights)


def unpack_kernel(place, *refs):
    direct, swapped, refs = refs[:PARTNERS], refs[PARTNERS : 2 * PARTNERS], refs[2 * PARTNERS :]
    own, (query_out, kept, sent, done) = (refs[:3], refs[3:6]), refs[6:]
    done[...] = jnp.zeros_like(done)
    wide = HEADS * HD

    def run(first, second):
        for side, (out, parts) in enumerate(((kept, first), (sent, second))):
            rows = slice(side * BLOCK, (side + 1) * BLOCK)
            query, key, value = own[side]
            query_out[rows, :wide] = query[...]
            out[:, :HD] = key[...]
            out[:, HD : 2 * HD] = value[...]
            for index, part in enumerate(parts):
                query_out[rows, (index + 1) * wide : (index + 2) * wide] = part[:, :wide]
                out[:, (index + 1) * 2 * HD : (index + 2) * 2 * HD] = part[:, wide:]

    @pl.when(place[1] == 0)
    def _():
        run(direct, swapped)

    @pl.when(place[1] == 1)
    def _():
        run(swapped, direct)


def unpack_weights(place, weights, direct, swapped):
    part = pl.BlockSpec((BLOCK, (HEADS + 2) * HD), lambda step, place: (0, 0))
    kept = [pl.BlockSpec((BLOCK, weight.shape[1]), lambda step, place: (place[0], 0)) for weight in weights]
    sent = [pl.BlockSpec((BLOCK, weight.shape[1]), lambda step, place: (place[0] ^ OTHER, 0)) for weight in weights]
    near = (BLOCK, (PARTNERS + 1) * 2 * HD)
    shapes = [(2 * BLOCK, (PARTNERS + 1) * HEADS * HD), near, near, (16, HD)]
    return pl.pallas_call(
        unpack_kernel,
        grid_spec=pltpu.PrefetchScalarGridSpec(
            num_scalar_prefetch=1,
            grid=(1,),
            in_specs=[part] * (2 * PARTNERS) + kept + sent,
            out_specs=[pl.BlockSpec(shape, lambda step, place: (0, 0)) for shape in shapes],
        ),
        out_shape=[jax.ShapeDtypeStruct(shape, BF) for shape in shapes],
        cost_estimate=cost(0, 4 * sum(rows * cols for rows, cols in shapes)),
        compiler_params=pltpu.CompilerParams(vmem_limit_bytes=32 * MIB),
    )(place, *direct, *swapped, *weights, *weights)


def join_queries_kernel(*refs):
    out = refs[-1]
    for index, part in enumerate(refs[: PARTNERS + 1]):
        out[:, index * HEADS * HD : (index + 1) * HEADS * HD] = part[...]


def join_queries(parts, after):
    shape = (BLOCK, (PARTNERS + 1) * HEADS * HD)
    whole = lambda shape: pl.BlockSpec(shape, lambda step: (0, 0))
    return pl.pallas_call(
        join_queries_kernel,
        grid=(1,),
        in_specs=[whole(part.shape) for part in parts] + [pl.BlockSpec(memory_space=pl.ANY)],
        out_specs=whole(shape),
        out_shape=jax.ShapeDtypeStruct(shape, BF),
        cost_estimate=cost(0, 4 * shape[0] * shape[1]),
        compiler_params=pltpu.CompilerParams(vmem_limit_bytes=12 * MIB),
    )(*parts, after)


def cost(flops, size):
    return pl.CostEstimate(flops=flops, bytes_accessed=size, transcendentals=0)


def over_x(value, partner):
    return lax.ppermute(value, "grp", [(source, source ^ partner) for source in range(GROUPS)])


def gather_over_x(value):
    return [value] + [over_x(value, partner) for partner in range(1, PARTNERS + 1)]


def product(left, right):
    return lax.dot_general(left, right, NT, preferred_element_type=F32)


def on_device(
    queries, key_rows, value_rows, output_rows, output_grad, log_normalizer, selection,
    query_weight, key_weight, value_weight,
):
    smem = pl.BlockSpec(memory_space=pltpu.SMEM)
    vmem = pl.BlockSpec(memory_space=pltpu.VMEM)
    hbm = pl.BlockSpec(memory_space=pl.ANY)
    small, large = [pltpu.CompilerParams(vmem_limit_bytes=size * MIB) for size in (4, 24)]
    index = lax.axis_index("ctx").astype(jnp.int32)
    place = index.reshape(1)
    group = jnp.stack([lax.axis_index("grp").astype(jnp.int32), index % 2])
    count = lax.axis_size("ctx")
    norm = log_normalizer.T.reshape(HEADS, 1, BLOCK)
    rows, pieces_shape = (BLOCK, 2 * HD), (BLOCKS, SLOTS, PIECE, 2 * HD)
    tile_flops = 10 * HEADS * HD * BLOCK * BLOCK

    own = pl.pallas_call(
        join_kernel,
        in_specs=[vmem, vmem],
        out_specs=vmem,
        out_shape=jax.ShapeDtypeStruct(rows, BF),
        cost_estimate=cost(0, 8 * BLOCK * HD),
        compiler_params=small,
    )(key_rows, value_rows)
    weights = (query_weight, key_weight, value_weight)
    packed = [pack_weights(group, partner, *weights) for partner in range(1, PARTNERS + 1)]
    direct = [over_x(part, index + 1) for index, part in enumerate(packed)]
    before = lax.ppermute(own, "ctx", [(i, (i + 1) % count) for i in range(count)])
    pieces = lax.all_to_all(own.reshape(BLOCKS, PIECE, 2 * HD), "ctx", 0, 0)
    picked = pl.pallas_call(
        pick_kernel,
        in_specs=[smem, vmem] + [hbm] * PARTNERS,
        out_specs=vmem,
        out_shape=jax.ShapeDtypeStruct(pieces_shape, BF),
        cost_estimate=cost(0, 12 * BLOCK * HD),
        compiler_params=small,
    )(selection, pieces, *packed)
    chosen = lax.all_to_all(picked, "ctx", 0, 0)

    whole = lambda shape: pl.BlockSpec(shape, lambda step: (0,) * len(shape))
    near_in = (queries, output_grad, output_rows, norm, own, before)
    delta, query_near, own_grad, before_grad = pl.pallas_call(
        near_kernel,
        grid=(1,),
        in_specs=[smem] + [whole(array.shape) for array in near_in],
        out_specs=[whole((HEADS, 1, BLOCK)), whole((HEADS, HD, BLOCK)), whole(rows), whole(rows)],
        out_shape=[
            jax.ShapeDtypeStruct((HEADS, 1, BLOCK), F32),
            jax.ShapeDtypeStruct((HEADS, HD, BLOCK), F32),
            jax.ShapeDtypeStruct(rows, F32),
            jax.ShapeDtypeStruct(rows, BF),
        ],
        scratch_shapes=tile_scratch(0),
        cost_estimate=cost(6 * tile_flops, 1 << 22),
        compiler_params=large,
    )(place, *near_in)
    before_sum = lax.ppermute(before_grad, "ctx", [(i, (i - 1) % count) for i in range(count)])

    far_in = (queries, output_grad, norm, delta, query_near, chosen)
    query_grad, chosen_grad = pl.pallas_call(
        far_kernel,
        grid=(1,),
        in_specs=[smem, smem] + [whole(array.shape) for array in far_in],
        out_specs=[whole((BLOCK, HEADS * HD)), whole(pieces_shape)],
        out_shape=[
            jax.ShapeDtypeStruct((BLOCK, HEADS * HD), BF),
            jax.ShapeDtypeStruct(pieces_shape, BF),
        ],
        scratch_shapes=tile_scratch(1),
        cost_estimate=cost(6 * tile_flops, 1 << 22),
        compiler_params=large,
    )(place, selection, *far_in)

    returned = lax.all_to_all(chosen_grad, "ctx", 0, 0)
    *direct, query_grad = lax.optimization_barrier((*direct, query_grad))
    swapped = [lax.ppermute(part, "ctx", [(i, i ^ 1) for i in range(count)]) for part in direct]
    query_all_weight, near_kept, near_sent, done = unpack_weights(group, weights, direct, swapped)
    query_parts = gather_over_x(query_grad)
    collected = pl.pallas_call(
        collect_kernel,
        in_specs=[smem, vmem, hbm],
        out_specs=vmem,
        out_shape=jax.ShapeDtypeStruct((BLOCKS, PIECE, 2 * HD), BF),
        scratch_shapes=[pltpu.VMEM((BLOCKS, PIECE, 2 * HD), F32)],
        cost_estimate=cost(0, 12 * BLOCK * HD),
        compiler_params=small,
    )(selection, returned, done)
    part = product(join_queries(query_parts, collected), query_all_weight)
    kept_part, sent_part = part[:, :BLOCK], part[:, BLOCK:]
    chosen_sum = lax.all_to_all(collected, "ctx", 0, 0).reshape(rows)
    factor = jnp.where(lax.broadcasted_iota(jnp.int32, rows, 1) < HD, SCALE, 1.0)
    near_grad = ((own_grad + before_sum.astype(F32) + chosen_sum.astype(F32)) * factor).astype(BF)
    half = BLOCK // HALVES
    pairs = [(source, source ^ OTHER) for source in range(GROUPS)]
    near_parts = [gather_over_x(near_grad[i * half : (i + 1) * half]) for i in range(HALVES)]
    outs = []
    for i, near_all in enumerate(near_parts):
        some = slice(i * half, (i + 1) * half)
        near_all = jnp.concatenate(near_all, axis=1)
        sent = (sent_part[some] + product(near_all, near_sent)).astype(BF)
        got = lax.ppermute(sent, "grp", pairs)
        outs.append((kept_part[some] + product(near_all, near_kept) + got.astype(F32)).astype(BF))
    return jnp.concatenate(outs, axis=0)


def solution(mesh):
    tokens = P("ctx", "grp")
    return jax.shard_map(
        on_device,
        mesh=mesh,
        in_specs=(tokens,) * 6 + (P(),) + (P(None, "grp"),) * 3,
        out_specs=tokens,
        check_vma=False,
    )
```

```python
import jax
import jax.numpy as jnp
from jax import lax
from jax.experimental import pallas as pl
from jax.experimental.pallas import tpu as pltpu
from jax.sharding import PartitionSpec as P

HD = 128
HEADS = 4
BLOCK = 512
BLOCKS = 32
PIECE = BLOCK // BLOCKS
SLOTS = 2
GROUPS = 8
SCALE = float(HD) ** (-0.5)
LOG2E = 1.4426950408889634
BF = jnp.bfloat16
F32 = jnp.float32
VMEM_BYTES = 60 * 1024 * 1024
PARAMS = pltpu.CompilerParams(vmem_limit_bytes=VMEM_BYTES)


def params(mib):
    return pltpu.CompilerParams(vmem_limit_bytes=mib * 1024 * 1024)


PARTNERS = 3
HALVES = 2
TOKEN = (16, HD)
OTHER = 4

NT = (((1,), (1,)), ((), ()))


def others(selection, block):
    before = block - 1
    first, second, third = selection[block, 0], selection[block, 1], selection[block, 2]
    return jnp.where(first == before, second, first), jnp.where(third == before, second, third)


def pick_kernel(selection, pieces, *refs):
    out = refs[-1]

    def step(block, carry):
        for slot, chosen in enumerate(others(selection, block)):
            out[block, slot] = pieces[chosen]
        return carry

    lax.fori_loop(0, BLOCKS, step, 0, unroll=4)


def collect_kernel(selection, parts, *refs):
    out, total = refs[-2:]
    total[...] = jnp.zeros_like(total)

    def step(block, carry):
        for slot, chosen in enumerate(others(selection, block)):

            @pl.when(chosen < block)
            def _():
                total[chosen] += parts[block, slot].astype(F32)

        return carry

    lax.fori_loop(0, BLOCKS, step, 0, unroll=4)
    out[...] = total[...].astype(BF)


def attend(queries, output_grad, norm, delta, scratch, causal):
    keys, values, keys_t, query_total, key_total, value_total = scratch
    key_total[...] = jnp.zeros_like(key_total)
    value_total[...] = jnp.zeros_like(value_total)
    key, value, key_t = keys[...], values[...], keys_t[...]

    def head_step(head, carry):
        cols = pl.ds(pl.multiple_of(head * HD, HD), HD)
        query, grad = queries[:, cols], output_grad[:, cols]
        scores = lax.dot_general(key, query, NT, preferred_element_type=F32)
        prob_grad = lax.dot_general(value, grad, NT, preferred_element_type=F32)
        probs = jnp.exp2(scores * (SCALE * LOG2E) - norm[head] * LOG2E)
        if causal:
            shape = (BLOCK, BLOCK)
            seen = lax.broadcasted_iota(jnp.int32, shape, 0) <= lax.broadcasted_iota(jnp.int32, shape, 1)
            probs = jnp.where(seen, probs, 0.0)
        score_half = (probs * (prob_grad - delta[head])).astype(BF)
        value_total[...] += jnp.dot(probs.astype(BF), grad, preferred_element_type=F32)
        key_total[...] += jnp.dot(score_half, query, preferred_element_type=F32)
        query_total[head] += jnp.dot(key_t, score_half, preferred_element_type=F32)
        return carry

    lax.fori_loop(0, HEADS, head_step, 0, unroll=True)


def load(scratch, key, value):
    keys, values, keys_t = scratch[:3]
    keys[...] = key
    values[...] = value
    keys_t[...] = key.astype(F32).T.astype(BF)


def near_kernel(
    place, queries, output_grad, output_rows, norm, own, before,
    delta, query_total, own_out, before_out, keys, values, keys_t, key_total, value_total,
):
    scratch = (keys, values, keys_t, query_total, key_total, value_total)
    for head in range(HEADS):
        cols = pl.ds(head * HD, HD)
        product = output_rows[:, cols].astype(F32) * output_grad[:, cols].astype(F32)
        delta[head] = jnp.sum(product.T, axis=0, keepdims=True)
    query_total[...] = jnp.zeros_like(query_total)
    load(scratch, own[:, :HD], own[:, HD:])
    attend(queries, output_grad, norm, delta, scratch, True)
    own_out[:, :HD] = key_total[...]
    own_out[:, HD:] = value_total[...]

    @pl.when(place[0] > 0)
    def _():
        load(scratch, before[:, :HD], before[:, HD:])
        attend(queries, output_grad, norm, delta, scratch, False)
        before_out[:, :HD] = key_total[...].astype(BF)
        before_out[:, HD:] = value_total[...].astype(BF)

    @pl.when(place[0] == 0)
    def _():
        before_out[...] = jnp.zeros_like(before_out)


def far_kernel(
    place, selection, queries, output_grad, norm, delta, query_near, chosen,
    query_out, chosen_out, done, keys, values, keys_t, query_total, key_total, value_total,
):
    done[...] = jnp.zeros_like(done)
    scratch = (keys, values, keys_t, query_total, key_total, value_total)
    block = place[0]
    query_total[...] = query_near[...]
    for slot, pick in enumerate(others(selection, block)):

        @pl.when(pick < block)
        def _():
            load(
                scratch,
                chosen[:, slot, :, :HD].reshape(BLOCK, HD),
                chosen[:, slot, :, HD:].reshape(BLOCK, HD),
            )
            attend(queries, output_grad, norm, delta, scratch, False)
            chosen_out[:, slot, :, :HD] = key_total[...].reshape(BLOCKS, PIECE, HD).astype(BF)
            chosen_out[:, slot, :, HD:] = value_total[...].reshape(BLOCKS, PIECE, HD).astype(BF)

        @pl.when(pick >= block)
        def _():
            chosen_out[:, slot] = jnp.zeros((BLOCKS, PIECE, 2 * HD), BF)

    for head in range(HEADS):
        query_out[:, head * HD : (head + 1) * HD] = (query_total[head].T * SCALE).astype(BF)


def tile_scratch(with_query):
    shapes = [((BLOCK, HD), BF), ((BLOCK, HD), BF), ((HD, BLOCK), BF)]
    shapes += [((HEADS, HD, BLOCK), F32)] * with_query + [((BLOCK, HD), F32)] * 2
    return [pltpu.VMEM(shape, dtype) for shape, dtype in shapes]


def join_kernel(key_rows, value_rows, out):
    out[:, :HD] = key_rows[...]
    out[:, HD:] = value_rows[...]


def pack_kernel(place, *refs):
    wide = HEADS * HD
    done = refs[-1]
    done[...] = jnp.zeros_like(done)
    for partner in range(PARTNERS):
        query, key, value = refs[3 * partner : 3 * partner + 3]
        out = refs[3 * PARTNERS + partner]
        out[:, :wide] = query[...]
        out[:, wide : wide + HD] = key[...]
        out[:, wide + HD :] = value[...]


def pack_weights(place, weights):
    steps = 4
    rows, width = BLOCK // steps, (HEADS + 2) * HD

    def index(partner):
        return lambda step, place: ((place[0] ^ (place[1] * OTHER) ^ partner) * steps + step, 0)

    partners = range(1, PARTNERS + 1)
    return pl.pallas_call(
        pack_kernel,
        grid_spec=pltpu.PrefetchScalarGridSpec(
            num_scalar_prefetch=1,
            grid=(steps,),
            in_specs=[
                pl.BlockSpec((rows, weight.shape[1]), index(partner)) for partner in partners for weight in weights
            ],
            out_specs=[pl.BlockSpec((rows, width), lambda step, place: (step, 0))] * PARTNERS
            + [pl.BlockSpec(TOKEN, lambda step, place: (0, 0))],
        ),
        out_shape=[jax.ShapeDtypeStruct((BLOCK, width), BF)] * PARTNERS + [jax.ShapeDtypeStruct(TOKEN, BF)],
        cost_estimate=cost(0, 4 * PARTNERS * BLOCK * width),
        compiler_params=PARAMS,
    )(place, *weights * PARTNERS)


def unpack_kernel(place, *refs):
    direct, swapped, refs = refs[:PARTNERS], refs[PARTNERS : 2 * PARTNERS], refs[2 * PARTNERS :]
    own, (query_out, kept, sent, done) = (refs[:3], refs[3:6]), refs[7:]
    done[...] = jnp.zeros_like(done)
    wide = HEADS * HD

    def run(first, second):
        for side, (out, parts) in enumerate(((kept, first), (sent, second))):
            rows = slice(side * BLOCK, (side + 1) * BLOCK)
            query, key, value = own[side]
            query_out[rows, :wide] = query[...]
            out[:, :HD] = key[...]
            out[:, HD : 2 * HD] = value[...]
            for index, part in enumerate(parts):
                query_out[rows, (index + 1) * wide : (index + 2) * wide] = part[:, :wide]
                out[:, (index + 1) * 2 * HD : (index + 2) * 2 * HD] = part[:, wide:]

    @pl.when(place[1] == 0)
    def _():
        run(direct, swapped)

    @pl.when(place[1] == 1)
    def _():
        run(swapped, direct)


def unpack_weights(place, weights, direct, swapped, after):
    part = pl.BlockSpec((BLOCK, (HEADS + 2) * HD), lambda step, place: (0, 0))
    kept = [pl.BlockSpec((BLOCK, weight.shape[1]), lambda step, place: (place[0], 0)) for weight in weights]
    sent = [pl.BlockSpec((BLOCK, weight.shape[1]), lambda step, place: (place[0] ^ OTHER, 0)) for weight in weights]
    near = (BLOCK, (PARTNERS + 1) * 2 * HD)
    shapes = [(2 * BLOCK, (PARTNERS + 1) * HEADS * HD), near, near, TOKEN]
    return pl.pallas_call(
        unpack_kernel,
        grid_spec=pltpu.PrefetchScalarGridSpec(
            num_scalar_prefetch=1,
            grid=(1,),
            in_specs=[part] * (2 * PARTNERS) + kept + sent + [pl.BlockSpec(memory_space=pl.ANY)],
            out_specs=[pl.BlockSpec(shape, lambda step, place: (0, 0)) for shape in shapes],
        ),
        out_shape=[jax.ShapeDtypeStruct(shape, BF) for shape in shapes],
        cost_estimate=cost(0, 4 * sum(rows * cols for rows, cols in shapes)),
        compiler_params=PARAMS,
    )(place, *direct, *swapped, *weights, *weights, after)


def join_queries_kernel(*refs):
    out = refs[-1]
    for index, part in enumerate(refs[: PARTNERS + 1]):
        out[:, index * HEADS * HD : (index + 1) * HEADS * HD] = part[...]


def join_queries(parts, after):
    shape = (BLOCK, (PARTNERS + 1) * HEADS * HD)
    whole = lambda shape: pl.BlockSpec(shape, lambda step: (0, 0))
    return pl.pallas_call(
        join_queries_kernel,
        grid=(1,),
        in_specs=[whole(part.shape) for part in parts] + [pl.BlockSpec(memory_space=pl.ANY)],
        out_specs=whole(shape),
        out_shape=jax.ShapeDtypeStruct(shape, BF),
        cost_estimate=cost(0, 4 * shape[0] * shape[1]),
        compiler_params=params(12),
    )(*parts, after)


def cost(flops, size):
    return pl.CostEstimate(flops=flops, bytes_accessed=size, transcendentals=0)


def over_x(value, partner):
    return lax.ppermute(value, "grp", [(source, source ^ partner) for source in range(GROUPS)])


def gather_over_x(value):
    return [value] + [over_x(value, partner) for partner in range(1, PARTNERS + 1)]


def product(left, right):
    return lax.dot_general(left, right, NT, preferred_element_type=F32)


def on_device(
    queries, key_rows, value_rows, output_rows, output_grad, log_normalizer, selection,
    query_weight, key_weight, value_weight,
):
    smem = pl.BlockSpec(memory_space=pltpu.SMEM)
    whole = lambda shape: pl.BlockSpec(shape, lambda step: (0,) * len(shape))
    hbm = pl.BlockSpec(memory_space=pl.ANY)
    index = lax.axis_index("ctx").astype(jnp.int32)
    place = index.reshape(1)
    group = jnp.stack([lax.axis_index("grp").astype(jnp.int32), index % 2])
    count = lax.axis_size("ctx")
    norm = log_normalizer.T.reshape(HEADS, 1, BLOCK)
    rows, pieces_shape = (BLOCK, 2 * HD), (BLOCKS, SLOTS, PIECE, 2 * HD)
    tile_flops = 10 * HEADS * HD * BLOCK * BLOCK

    own = pl.pallas_call(
        join_kernel,
        grid=(1,),
        in_specs=[whole(key_rows.shape), whole(value_rows.shape)],
        out_specs=whole(rows),
        out_shape=jax.ShapeDtypeStruct(rows, BF),
        cost_estimate=cost(0, 8 * BLOCK * HD),
        compiler_params=PARAMS,
    )(key_rows, value_rows)
    weights = (query_weight, key_weight, value_weight)
    *packed, pack_done = pack_weights(group, weights)
    direct = [over_x(part, index + 1) for index, part in enumerate(packed)]
    before = lax.ppermute(own, "ctx", [(i, (i + 1) % count) for i in range(count)])
    pieces = lax.all_to_all(own.reshape(BLOCKS, PIECE, 2 * HD), "ctx", 0, 0)
    picked = pl.pallas_call(
        pick_kernel,
        grid=(1,),
        in_specs=[smem, whole(pieces.shape), hbm],
        out_specs=whole(pieces_shape),
        out_shape=jax.ShapeDtypeStruct(pieces_shape, BF),
        cost_estimate=cost(0, 12 * BLOCK * HD),
        compiler_params=params(8),
    )(selection, pieces, pack_done)
    chosen = lax.all_to_all(picked, "ctx", 0, 0)

    near_in = (queries, output_grad, output_rows, norm, own, before)
    delta, query_near, own_grad, before_grad = pl.pallas_call(
        near_kernel,
        grid=(1,),
        in_specs=[smem] + [whole(array.shape) for array in near_in],
        out_specs=[whole((HEADS, 1, BLOCK)), whole((HEADS, HD, BLOCK)), whole(rows), whole(rows)],
        out_shape=[
            jax.ShapeDtypeStruct((HEADS, 1, BLOCK), F32),
            jax.ShapeDtypeStruct((HEADS, HD, BLOCK), F32),
            jax.ShapeDtypeStruct(rows, F32),
            jax.ShapeDtypeStruct(rows, BF),
        ],
        scratch_shapes=tile_scratch(0),
        cost_estimate=cost(600 * tile_flops, 1 << 22),
        compiler_params=PARAMS,
    )(place, *near_in)
    before_sum = lax.ppermute(before_grad, "ctx", [(i, (i - 1) % count) for i in range(count)])

    far_in = (queries, output_grad, norm, delta, query_near, chosen)
    query_grad, chosen_grad, far_done = pl.pallas_call(
        far_kernel,
        grid=(1,),
        in_specs=[smem, smem] + [whole(array.shape) for array in far_in],
        out_specs=[whole((BLOCK, HEADS * HD)), whole(pieces_shape), whole(TOKEN)],
        out_shape=[
            jax.ShapeDtypeStruct((BLOCK, HEADS * HD), BF),
            jax.ShapeDtypeStruct(pieces_shape, BF),
            jax.ShapeDtypeStruct(TOKEN, BF),
        ],
        scratch_shapes=tile_scratch(1),
        cost_estimate=cost(6 * tile_flops, 1 << 22),
        compiler_params=PARAMS,
    )(place, selection, *far_in)

    returned = lax.all_to_all(chosen_grad, "ctx", 0, 0)
    *direct, far_done = lax.optimization_barrier((*direct, far_done))
    swapped = [lax.ppermute(part, "ctx", [(i, i ^ 1) for i in range(count)]) for part in direct]
    query_all_weight, near_kept, near_sent, done = unpack_weights(group, weights, direct, swapped, far_done)
    query_parts = gather_over_x(query_grad)
    collected = pl.pallas_call(
        collect_kernel,
        grid=(1,),
        in_specs=[smem, whole(pieces_shape), hbm],
        out_specs=whole(pieces.shape),
        out_shape=jax.ShapeDtypeStruct((BLOCKS, PIECE, 2 * HD), BF),
        scratch_shapes=[pltpu.VMEM((BLOCKS, PIECE, 2 * HD), F32)],
        cost_estimate=cost(0, 12 * BLOCK * HD),
        compiler_params=params(8),
    )(selection, returned, done)
    part = product(join_queries(query_parts, collected), query_all_weight)
    kept_part, sent_part = part[:, :BLOCK], part[:, BLOCK:]
    chosen_sum = lax.all_to_all(collected, "ctx", 0, 0).reshape(rows)
    chosen_sum, kept_part, sent_part = lax.optimization_barrier((chosen_sum, kept_part, sent_part))
    factor = jnp.where(lax.broadcasted_iota(jnp.int32, rows, 1) < HD, SCALE, 1.0)
    near_grad = ((own_grad + before_sum.astype(F32) + chosen_sum.astype(F32)) * factor).astype(BF)
    half = BLOCK // HALVES
    pairs = [(source, source ^ OTHER) for source in range(GROUPS)]
    near_parts = [gather_over_x(near_grad[i * half : (i + 1) * half]) for i in range(HALVES)]
    kept, got = [], []
    for i, near_all in enumerate(near_parts):
        some = slice(i * half, (i + 1) * half)
        near_all = jnp.concatenate(near_all, axis=1)
        sent = (sent_part[some] + product(near_all, near_sent)).astype(BF)
        got.append(lax.ppermute(sent, "grp", pairs))
        kept.append(kept_part[some] + product(near_all, near_kept))
    kept = lax.optimization_barrier(kept)
    return jnp.concatenate([(part + other.astype(F32)).astype(BF) for part, other in zip(kept, got)], axis=0)


def solution(mesh):
    tokens = P("ctx", "grp")
    return jax.shard_map(
        on_device,
        mesh=mesh,
        in_specs=(tokens,) * 6 + (P(),) + (P(None, "grp"),) * 3,
        out_specs=tokens,
        check_vma=False,
    )
```

```python
import jax
import jax.numpy as jnp
from jax import lax
from jax.experimental import pallas as pl
from jax.experimental.pallas import tpu as pltpu
from jax.sharding import PartitionSpec as P

HD = 128
HEADS = 4
BLOCK = 512
BLOCKS = 32
PIECE = BLOCK // BLOCKS
SLOTS = 2
GROUPS = 8
SCALE = float(HD) ** (-0.5)
LOG2E = 1.4426950408889634
BF = jnp.bfloat16
F32 = jnp.float32
VMEM_BYTES = 60 * 1024 * 1024
PARAMS = pltpu.CompilerParams(vmem_limit_bytes=VMEM_BYTES)


def params(mib):
    return pltpu.CompilerParams(vmem_limit_bytes=mib * 1024 * 1024)


PARTNERS = 3
HALVES = 2
TOKEN = (16, HD)
OTHER = 4

NT = (((1,), (1,)), ((), ()))


def others(selection, block):
    before = block - 1
    first, second, third = selection[block, 0], selection[block, 1], selection[block, 2]
    return jnp.where(first == before, second, first), jnp.where(third == before, second, third)


def pick_kernel(selection, pieces, *refs):
    out = refs[-1]

    def step(block, carry):
        for slot, chosen in enumerate(others(selection, block)):
            out[block, slot] = pieces[chosen]
        return carry

    lax.fori_loop(0, BLOCKS, step, 0, unroll=4)


def collect_kernel(selection, parts, *refs):
    out, total = refs[-2:]
    total[...] = jnp.zeros_like(total)

    def step(block, carry):
        for slot, chosen in enumerate(others(selection, block)):

            @pl.when(chosen < block)
            def _():
                total[chosen] += parts[block, slot].astype(F32)

        return carry

    lax.fori_loop(0, BLOCKS, step, 0, unroll=4)
    out[...] = total[...].astype(BF)


def attend(queries, output_grad, norm, delta, scratch, causal):
    keys, values, keys_t, query_total, key_total, value_total = scratch
    key_total[...] = jnp.zeros_like(key_total)
    value_total[...] = jnp.zeros_like(value_total)
    key, value, key_t = keys[...], values[...], keys_t[...]

    def head_step(head, carry):
        cols = pl.ds(pl.multiple_of(head * HD, HD), HD)
        query, grad = queries[:, cols], output_grad[:, cols]
        scores = lax.dot_general(key, query, NT, preferred_element_type=F32)
        prob_grad = lax.dot_general(value, grad, NT, preferred_element_type=F32)
        probs = jnp.exp2(scores * (SCALE * LOG2E) - norm[head] * LOG2E)
        if causal:
            shape = (BLOCK, BLOCK)
            seen = lax.broadcasted_iota(jnp.int32, shape, 0) <= lax.broadcasted_iota(jnp.int32, shape, 1)
            probs = jnp.where(seen, probs, 0.0)
        score_half = (probs * (prob_grad - delta[head])).astype(BF)
        value_total[...] += jnp.dot(probs.astype(BF), grad, preferred_element_type=F32)
        key_total[...] += jnp.dot(score_half, query, preferred_element_type=F32)
        query_total[head] += jnp.dot(key_t, score_half, preferred_element_type=F32)
        return carry

    lax.fori_loop(0, HEADS, head_step, 0, unroll=True)


def load(scratch, key, value):
    keys, values, keys_t = scratch[:3]
    keys[...] = key
    values[...] = value
    keys_t[...] = key.astype(F32).T.astype(BF)


def near_kernel(
    place, queries, output_grad, output_rows, norm, own, before,
    delta, query_total, own_out, before_out, keys, values, keys_t, key_total, value_total,
):
    scratch = (keys, values, keys_t, query_total, key_total, value_total)
    for head in range(HEADS):
        cols = pl.ds(head * HD, HD)
        product = output_rows[:, cols].astype(F32) * output_grad[:, cols].astype(F32)
        delta[head] = jnp.sum(product.T, axis=0, keepdims=True)
    query_total[...] = jnp.zeros_like(query_total)
    load(scratch, own[:, :HD], own[:, HD:])
    attend(queries, output_grad, norm, delta, scratch, True)
    own_out[:, :HD] = key_total[...]
    own_out[:, HD:] = value_total[...]

    @pl.when(place[0] > 0)
    def _():
        load(scratch, before[:, :HD], before[:, HD:])
        attend(queries, output_grad, norm, delta, scratch, False)
        before_out[:, :HD] = key_total[...].astype(BF)
        before_out[:, HD:] = value_total[...].astype(BF)

    @pl.when(place[0] == 0)
    def _():
        before_out[...] = jnp.zeros_like(before_out)


def far_kernel(
    place, selection, queries, output_grad, norm, delta, query_near, chosen,
    query_out, chosen_out, done, keys, values, keys_t, query_total, key_total, value_total,
):
    done[...] = jnp.zeros_like(done)
    scratch = (keys, values, keys_t, query_total, key_total, value_total)
    block = place[0]
    query_total[...] = query_near[...]
    for slot, pick in enumerate(others(selection, block)):

        @pl.when(pick < block)
        def _():
            load(
                scratch,
                chosen[:, slot, :, :HD].reshape(BLOCK, HD),
                chosen[:, slot, :, HD:].reshape(BLOCK, HD),
            )
            attend(queries, output_grad, norm, delta, scratch, False)
            chosen_out[:, slot, :, :HD] = key_total[...].reshape(BLOCKS, PIECE, HD).astype(BF)
            chosen_out[:, slot, :, HD:] = value_total[...].reshape(BLOCKS, PIECE, HD).astype(BF)

        @pl.when(pick >= block)
        def _():
            chosen_out[:, slot] = jnp.zeros((BLOCKS, PIECE, 2 * HD), BF)

    for head in range(HEADS):
        query_out[:, head * HD : (head + 1) * HD] = (query_total[head].T * SCALE).astype(BF)


def tile_scratch(with_query):
    shapes = [((BLOCK, HD), BF), ((BLOCK, HD), BF), ((HD, BLOCK), BF)]
    shapes += [((HEADS, HD, BLOCK), F32)] * with_query + [((BLOCK, HD), F32)] * 2
    return [pltpu.VMEM(shape, dtype) for shape, dtype in shapes]


def join_kernel(key_rows, value_rows, out):
    out[:, :HD] = key_rows[...]
    out[:, HD:] = value_rows[...]


def pack_kernel(place, *refs):
    wide = HEADS * HD
    done = refs[-1]
    done[...] = jnp.zeros_like(done)
    for partner in range(PARTNERS):
        query, key, value = refs[3 * partner : 3 * partner + 3]
        out = refs[3 * PARTNERS + partner]
        out[:, :wide] = query[...]
        out[:, wide : wide + HD] = key[...]
        out[:, wide + HD :] = value[...]


def pack_weights(place, weights):
    steps = 4
    rows, width = BLOCK // steps, (HEADS + 2) * HD

    def index(partner):
        return lambda step, place: ((place[0] ^ (place[1] * OTHER) ^ partner) * steps + step, 0)

    partners = range(1, PARTNERS + 1)
    return pl.pallas_call(
        pack_kernel,
        grid_spec=pltpu.PrefetchScalarGridSpec(
            num_scalar_prefetch=1,
            grid=(steps,),
            in_specs=[
                pl.BlockSpec((rows, weight.shape[1]), index(partner)) for partner in partners for weight in weights
            ],
            out_specs=[pl.BlockSpec((rows, width), lambda step, place: (step, 0))] * PARTNERS
            + [pl.BlockSpec(TOKEN, lambda step, place: (0, 0))],
        ),
        out_shape=[jax.ShapeDtypeStruct((BLOCK, width), BF)] * PARTNERS + [jax.ShapeDtypeStruct(TOKEN, BF)],
        cost_estimate=cost(0, 4 * PARTNERS * BLOCK * width),
        compiler_params=PARAMS,
    )(place, *weights * PARTNERS)


def unpack_kernel(place, *refs):
    direct, swapped, refs = refs[:PARTNERS], refs[PARTNERS : 2 * PARTNERS], refs[2 * PARTNERS :]
    own, (query_out, kept, sent, done) = (refs[:3], refs[3:6]), refs[7:]
    done[...] = jnp.zeros_like(done)
    wide = HEADS * HD

    def run(first, second):
        for side, (out, parts) in enumerate(((kept, first), (sent, second))):
            rows = slice(side * BLOCK, (side + 1) * BLOCK)
            query, key, value = own[side]
            query_out[rows, :wide] = query[...]
            out[:, :HD] = key[...]
            out[:, HD : 2 * HD] = value[...]
            for index, part in enumerate(parts):
                query_out[rows, (index + 1) * wide : (index + 2) * wide] = part[:, :wide]
                out[:, (index + 1) * 2 * HD : (index + 2) * 2 * HD] = part[:, wide:]

    @pl.when(place[1] == 0)
    def _():
        run(direct, swapped)

    @pl.when(place[1] == 1)
    def _():
        run(swapped, direct)


def unpack_weights(place, weights, direct, swapped, after):
    part = pl.BlockSpec((BLOCK, (HEADS + 2) * HD), lambda step, place: (0, 0))
    kept = [pl.BlockSpec((BLOCK, weight.shape[1]), lambda step, place: (place[0], 0)) for weight in weights]
    sent = [pl.BlockSpec((BLOCK, weight.shape[1]), lambda step, place: (place[0] ^ OTHER, 0)) for weight in weights]
    near = (BLOCK, (PARTNERS + 1) * 2 * HD)
    shapes = [(2 * BLOCK, (PARTNERS + 1) * HEADS * HD), near, near, TOKEN]
    return pl.pallas_call(
        unpack_kernel,
        grid_spec=pltpu.PrefetchScalarGridSpec(
            num_scalar_prefetch=1,
            grid=(1,),
            in_specs=[part] * (2 * PARTNERS) + kept + sent + [pl.BlockSpec(memory_space=pl.ANY)],
            out_specs=[pl.BlockSpec(shape, lambda step, place: (0, 0)) for shape in shapes],
        ),
        out_shape=[jax.ShapeDtypeStruct(shape, BF) for shape in shapes],
        cost_estimate=cost(0, 4 * sum(rows * cols for rows, cols in shapes)),
        compiler_params=PARAMS,
    )(place, *direct, *swapped, *weights, *weights, after)


def join_queries_kernel(*refs):
    out = refs[-1]
    for index, part in enumerate(refs[: PARTNERS + 1]):
        out[:, index * HEADS * HD : (index + 1) * HEADS * HD] = part[...]


def join_queries(parts, after):
    shape = (BLOCK, (PARTNERS + 1) * HEADS * HD)
    whole = lambda shape: pl.BlockSpec(shape, lambda step: (0, 0))
    return pl.pallas_call(
        join_queries_kernel,
        grid=(1,),
        in_specs=[whole(part.shape) for part in parts] + [pl.BlockSpec(memory_space=pl.ANY)],
        out_specs=whole(shape),
        out_shape=jax.ShapeDtypeStruct(shape, BF),
        cost_estimate=cost(0, 4 * shape[0] * shape[1]),
        compiler_params=params(12),
    )(*parts, after)


def cost(flops, size):
    return pl.CostEstimate(flops=flops, bytes_accessed=size, transcendentals=0)


def over_x(value, partner):
    return lax.ppermute(value, "grp", [(source, source ^ partner) for source in range(GROUPS)])


def gather_over_x(value):
    return [value] + [over_x(value, partner) for partner in range(1, PARTNERS + 1)]


def product(left, right):
    return lax.dot_general(left, right, NT, preferred_element_type=F32)


def on_device(
    queries, key_rows, value_rows, output_rows, output_grad, log_normalizer, selection,
    query_weight, key_weight, value_weight,
):
    smem = pl.BlockSpec(memory_space=pltpu.SMEM)
    whole = lambda shape: pl.BlockSpec(shape, lambda step: (0,) * len(shape))
    hbm = pl.BlockSpec(memory_space=pl.ANY)
    index = lax.axis_index("ctx").astype(jnp.int32)
    place = index.reshape(1)
    group = jnp.stack([lax.axis_index("grp").astype(jnp.int32), index % 2])
    count = lax.axis_size("ctx")
    norm = log_normalizer.T.reshape(HEADS, 1, BLOCK)
    rows, pieces_shape = (BLOCK, 2 * HD), (BLOCKS, SLOTS, PIECE, 2 * HD)
    tile_flops = 10 * HEADS * HD * BLOCK * BLOCK

    own = pl.pallas_call(
        join_kernel,
        grid=(1,),
        in_specs=[whole(key_rows.shape), whole(value_rows.shape)],
        out_specs=whole(rows),
        out_shape=jax.ShapeDtypeStruct(rows, BF),
        cost_estimate=cost(0, 8 * BLOCK * HD),
        compiler_params=PARAMS,
    )(key_rows, value_rows)
    weights = (query_weight, key_weight, value_weight)
    *packed, pack_done = pack_weights(group, weights)
    direct = [over_x(part, index + 1) for index, part in enumerate(packed)]
    before = lax.ppermute(own, "ctx", [(i, (i + 1) % count) for i in range(count)])
    pieces = lax.all_to_all(own.reshape(BLOCKS, PIECE, 2 * HD), "ctx", 0, 0)
    picked = pl.pallas_call(
        pick_kernel,
        grid=(1,),
        in_specs=[smem, whole(pieces.shape)],
        out_specs=whole(pieces_shape),
        out_shape=jax.ShapeDtypeStruct(pieces_shape, BF),
        cost_estimate=cost(0, 12 * BLOCK * HD),
        compiler_params=params(8),
    )(selection, pieces)
    chosen = lax.all_to_all(picked, "ctx", 0, 0)

    near_in = (queries, output_grad, output_rows, norm, own, before)
    delta, query_near, own_grad, before_grad = pl.pallas_call(
        near_kernel,
        grid=(1,),
        in_specs=[smem] + [whole(array.shape) for array in near_in],
        out_specs=[whole((HEADS, 1, BLOCK)), whole((HEADS, HD, BLOCK)), whole(rows), whole(rows)],
        out_shape=[
            jax.ShapeDtypeStruct((HEADS, 1, BLOCK), F32),
            jax.ShapeDtypeStruct((HEADS, HD, BLOCK), F32),
            jax.ShapeDtypeStruct(rows, F32),
            jax.ShapeDtypeStruct(rows, BF),
        ],
        scratch_shapes=tile_scratch(0),
        cost_estimate=cost(600 * tile_flops, 1 << 22),
        compiler_params=PARAMS,
    )(place, *near_in)
    before_sum = lax.ppermute(before_grad, "ctx", [(i, (i - 1) % count) for i in range(count)])

    far_in = (queries, output_grad, norm, delta, query_near, chosen)
    query_grad, chosen_grad, far_done = pl.pallas_call(
        far_kernel,
        grid=(1,),
        in_specs=[smem, smem] + [whole(array.shape) for array in far_in],
        out_specs=[whole((BLOCK, HEADS * HD)), whole(pieces_shape), whole(TOKEN)],
        out_shape=[
            jax.ShapeDtypeStruct((BLOCK, HEADS * HD), BF),
            jax.ShapeDtypeStruct(pieces_shape, BF),
            jax.ShapeDtypeStruct(TOKEN, BF),
        ],
        scratch_shapes=tile_scratch(1),
        cost_estimate=cost(6 * tile_flops, 1 << 22),
        compiler_params=PARAMS,
    )(place, selection, *far_in)

    returned = lax.all_to_all(chosen_grad, "ctx", 0, 0)
    *direct, far_done = lax.optimization_barrier((*direct, far_done))
    swapped = [lax.ppermute(part, "ctx", [(i, i ^ 1) for i in range(count)]) for part in direct]
    query_all_weight, near_kept, near_sent, done = unpack_weights(group, weights, direct, swapped, far_done)
    query_parts = gather_over_x(query_grad)
    collected = pl.pallas_call(
        collect_kernel,
        grid=(1,),
        in_specs=[smem, whole(pieces_shape)],
        out_specs=whole(pieces.shape),
        out_shape=jax.ShapeDtypeStruct((BLOCKS, PIECE, 2 * HD), BF),
        scratch_shapes=[pltpu.VMEM((BLOCKS, PIECE, 2 * HD), F32)],
        cost_estimate=cost(0, 12 * BLOCK * HD),
        compiler_params=params(8),
    )(selection, returned)
    part = product(join_queries(query_parts, collected), query_all_weight)
    kept_part, sent_part = part[:, :BLOCK], part[:, BLOCK:]
    chosen_sum = lax.all_to_all(collected, "ctx", 0, 0).reshape(rows)
    chosen_sum, kept_part, sent_part = lax.optimization_barrier((chosen_sum, kept_part, sent_part))
    factor = jnp.where(lax.broadcasted_iota(jnp.int32, rows, 1) < HD, SCALE, 1.0)
    near_grad = ((own_grad + before_sum.astype(F32) + chosen_sum.astype(F32)) * factor).astype(BF)
    half = BLOCK // HALVES
    pairs = [(source, source ^ OTHER) for source in range(GROUPS)]
    near_parts = [gather_over_x(near_grad[i * half : (i + 1) * half]) for i in range(HALVES)]
    kept, got = [], []
    for i, near_all in enumerate(near_parts):
        some = slice(i * half, (i + 1) * half)
        near_all = jnp.concatenate(near_all, axis=1)
        sent = (sent_part[some] + product(near_all, near_sent)).astype(BF)
        got.append(lax.ppermute(sent, "grp", pairs))
        kept.append(kept_part[some] + product(near_all, near_kept))
    kept = lax.optimization_barrier(kept)
    return jnp.concatenate([(part + other.astype(F32)).astype(BF) for part, other in zip(kept, got)], axis=0)


def solution(mesh):
    tokens = P("ctx", "grp")
    return jax.shard_map(
        on_device,
        mesh=mesh,
        in_specs=(tokens,) * 6 + (P(),) + (P(None, "grp"),) * 3,
        out_specs=tokens,
        check_vma=False,
    )
```

```python
import jax
import jax.numpy as jnp
from jax import lax
from jax.experimental import pallas as pl
from jax.experimental.pallas import tpu as pltpu
from jax.sharding import PartitionSpec as P

HD = 128
HEADS = 4
BLOCK = 512
BLOCKS = 32
PIECE = BLOCK // BLOCKS
SLOTS = 2
GROUPS = 8
SCALE = float(HD) ** (-0.5)
LOG2E = 1.4426950408889634
BF = jnp.bfloat16
F32 = jnp.float32
VMEM_BYTES = 60 * 1024 * 1024
PARAMS = pltpu.CompilerParams(vmem_limit_bytes=VMEM_BYTES)


def params(mib):
    return pltpu.CompilerParams(vmem_limit_bytes=mib * 1024 * 1024)


PARTNERS = 3
HALVES = 2
TOKEN = (16, HD)
OTHER = 4

NT = (((1,), (1,)), ((), ()))


def others(selection, block):
    before = block - 1
    first, second, third = selection[block, 0], selection[block, 1], selection[block, 2]
    return jnp.where(first == before, second, first), jnp.where(third == before, second, third)


def pick_kernel(selection, pieces, *refs):
    out = refs[-1]

    def step(block, carry):
        for slot, chosen in enumerate(others(selection, block)):
            out[block, slot] = pieces[chosen]
        return carry

    lax.fori_loop(0, BLOCKS, step, 0, unroll=True)


def collect_kernel(selection, parts, *refs):
    out, total = refs[-2:]
    total[...] = jnp.zeros_like(total)

    def step(block, carry):
        for slot, chosen in enumerate(others(selection, block)):
            total[chosen] += jnp.where(chosen < block, parts[block, slot].astype(F32), 0.0)

        return carry

    lax.fori_loop(0, BLOCKS, step, 0, unroll=8)
    out[...] = total[...].astype(BF)


def attend(queries, output_grad, norm, delta, scratch, causal):
    keys, values, keys_t, query_total, key_total, value_total = scratch
    key_total[...] = jnp.zeros_like(key_total)
    value_total[...] = jnp.zeros_like(value_total)
    key, value, key_t = keys[...], values[...], keys_t[...]

    def head_step(head, carry):
        cols = pl.ds(pl.multiple_of(head * HD, HD), HD)
        query, grad = queries[:, cols], output_grad[:, cols]
        scores = lax.dot_general(key, query, NT, preferred_element_type=F32)
        prob_grad = lax.dot_general(value, grad, NT, preferred_element_type=F32)
        probs = jnp.exp2(scores * (SCALE * LOG2E) - norm[head] * LOG2E)
        if causal:
            shape = (BLOCK, BLOCK)
            seen = lax.broadcasted_iota(jnp.int32, shape, 0) <= lax.broadcasted_iota(jnp.int32, shape, 1)
            probs = jnp.where(seen, probs, 0.0)
        score_half = (probs * (prob_grad - delta[head])).astype(BF)
        value_total[...] += jnp.dot(probs.astype(BF), grad, preferred_element_type=F32)
        key_total[...] += jnp.dot(score_half, query, preferred_element_type=F32)
        query_total[head] += jnp.dot(key_t, score_half, preferred_element_type=F32)
        return carry

    lax.fori_loop(0, HEADS, head_step, 0, unroll=True)


def load(scratch, key, value):
    keys, values, keys_t = scratch[:3]
    keys[...] = key
    values[...] = value
    keys_t[...] = key.astype(F32).T.astype(BF)


def near_kernel(
    place, queries, output_grad, output_rows, norm, own, before,
    delta, query_total, own_out, before_out, keys, values, keys_t, key_total, value_total,
):
    scratch = (keys, values, keys_t, query_total, key_total, value_total)
    for head in range(HEADS):
        cols = pl.ds(head * HD, HD)
        product = output_rows[:, cols].astype(F32) * output_grad[:, cols].astype(F32)
        delta[head] = jnp.sum(product.T, axis=0, keepdims=True)
    query_total[...] = jnp.zeros_like(query_total)
    load(scratch, own[:, :HD], own[:, HD:])
    attend(queries, output_grad, norm, delta, scratch, True)
    own_out[:, :HD] = key_total[...]
    own_out[:, HD:] = value_total[...]

    @pl.when(place[0] > 0)
    def _():
        load(scratch, before[:, :HD], before[:, HD:])
        attend(queries, output_grad, norm, delta, scratch, False)
        before_out[:, :HD] = key_total[...].astype(BF)
        before_out[:, HD:] = value_total[...].astype(BF)

    @pl.when(place[0] == 0)
    def _():
        before_out[...] = jnp.zeros_like(before_out)


def far_kernel(
    place, selection, queries, output_grad, norm, delta, query_near, chosen,
    query_out, chosen_out, done, keys, values, keys_t, query_total, key_total, value_total,
):
    done[...] = jnp.zeros_like(done)
    scratch = (keys, values, keys_t, query_total, key_total, value_total)
    block = place[0]
    query_total[...] = query_near[...]
    for slot, pick in enumerate(others(selection, block)):

        @pl.when(pick < block)
        def _():
            load(
                scratch,
                chosen[:, slot, :, :HD].reshape(BLOCK, HD),
                chosen[:, slot, :, HD:].reshape(BLOCK, HD),
            )
            attend(queries, output_grad, norm, delta, scratch, False)
            chosen_out[:, slot, :, :HD] = key_total[...].reshape(BLOCKS, PIECE, HD).astype(BF)
            chosen_out[:, slot, :, HD:] = value_total[...].reshape(BLOCKS, PIECE, HD).astype(BF)

        @pl.when(pick >= block)
        def _():
            chosen_out[:, slot] = jnp.zeros((BLOCKS, PIECE, 2 * HD), BF)

    for head in range(HEADS):
        query_out[:, head * HD : (head + 1) * HD] = (query_total[head].T * SCALE).astype(BF)


def tile_scratch(with_query):
    shapes = [((BLOCK, HD), BF), ((BLOCK, HD), BF), ((HD, BLOCK), BF)]
    shapes += [((HEADS, HD, BLOCK), F32)] * with_query + [((BLOCK, HD), F32)] * 2
    return [pltpu.VMEM(shape, dtype) for shape, dtype in shapes]


def join_kernel(key_rows, value_rows, out):
    out[:, :HD] = key_rows[...]
    out[:, HD:] = value_rows[...]


def pack_kernel(place, *refs):
    wide = HEADS * HD
    done = refs[-1]
    done[...] = jnp.zeros_like(done)
    for partner in range(PARTNERS):
        query, key, value = refs[3 * partner : 3 * partner + 3]
        out = refs[3 * PARTNERS + partner]
        out[:, :wide] = query[...]
        out[:, wide : wide + HD] = key[...]
        out[:, wide + HD :] = value[...]


def pack_weights(place, weights):
    steps = 2
    rows, width = BLOCK // steps, (HEADS + 2) * HD

    def index(partner):
        return lambda step, place: ((place[0] ^ (place[1] * OTHER) ^ partner) * steps + step, 0)

    partners = range(1, PARTNERS + 1)
    return pl.pallas_call(
        pack_kernel,
        grid_spec=pltpu.PrefetchScalarGridSpec(
            num_scalar_prefetch=1,
            grid=(steps,),
            in_specs=[
                pl.BlockSpec((rows, weight.shape[1]), index(partner)) for partner in partners for weight in weights
            ],
            out_specs=[pl.BlockSpec((rows, width), lambda step, place: (step, 0))] * PARTNERS
            + [pl.BlockSpec(TOKEN, lambda step, place: (0, 0))],
        ),
        out_shape=[jax.ShapeDtypeStruct((BLOCK, width), BF)] * PARTNERS + [jax.ShapeDtypeStruct(TOKEN, BF)],
        cost_estimate=cost(0, 4 * PARTNERS * BLOCK * width),
        compiler_params=PARAMS,
    )(place, *weights * PARTNERS)


def unpack_kernel(place, *refs):
    direct, swapped, refs = refs[:PARTNERS], refs[PARTNERS : 2 * PARTNERS], refs[2 * PARTNERS :]
    own, (query_out, kept, sent, done) = (refs[:3], refs[3:6]), refs[7:]
    done[...] = jnp.zeros_like(done)
    wide = HEADS * HD

    def run(first, second):
        for side, (out, parts) in enumerate(((kept, first), (sent, second))):
            rows = slice(side * BLOCK, (side + 1) * BLOCK)
            query, key, value = own[side]
            query_out[rows, :wide] = query[...]
            out[:, :HD] = key[...]
            out[:, HD : 2 * HD] = value[...]
            for index, part in enumerate(parts):
                query_out[rows, (index + 1) * wide : (index + 2) * wide] = part[:, :wide]
                out[:, (index + 1) * 2 * HD : (index + 2) * 2 * HD] = part[:, wide:]

    @pl.when(place[1] == 0)
    def _():
        run(direct, swapped)

    @pl.when(place[1] == 1)
    def _():
        run(swapped, direct)


def unpack_weights(place, weights, direct, swapped, after):
    part = pl.BlockSpec((BLOCK, (HEADS + 2) * HD), lambda step, place: (0, 0))
    kept = [pl.BlockSpec((BLOCK, weight.shape[1]), lambda step, place: (place[0], 0)) for weight in weights]
    sent = [pl.BlockSpec((BLOCK, weight.shape[1]), lambda step, place: (place[0] ^ OTHER, 0)) for weight in weights]
    near = (BLOCK, (PARTNERS + 1) * 2 * HD)
    shapes = [(2 * BLOCK, (PARTNERS + 1) * HEADS * HD), near, near, TOKEN]
    return pl.pallas_call(
        unpack_kernel,
        grid_spec=pltpu.PrefetchScalarGridSpec(
            num_scalar_prefetch=1,
            grid=(1,),
            in_specs=[part] * (2 * PARTNERS) + kept + sent + [pl.BlockSpec(memory_space=pl.ANY)],
            out_specs=[pl.BlockSpec(shape, lambda step, place: (0, 0)) for shape in shapes],
        ),
        out_shape=[jax.ShapeDtypeStruct(shape, BF) for shape in shapes],
        cost_estimate=cost(0, 4 * sum(rows * cols for rows, cols in shapes)),
        compiler_params=PARAMS,
    )(place, *direct, *swapped, *weights, *weights, after)


def join_queries_kernel(*refs):
    out = refs[-1]
    for index, part in enumerate(refs[: PARTNERS + 1]):
        out[:, index * HEADS * HD : (index + 1) * HEADS * HD] = part[...]


def join_queries(parts, after):
    shape = (BLOCK, (PARTNERS + 1) * HEADS * HD)
    whole = lambda shape: pl.BlockSpec(shape, lambda step: (0, 0))
    return pl.pallas_call(
        join_queries_kernel,
        grid=(1,),
        in_specs=[whole(part.shape) for part in parts] + [pl.BlockSpec(memory_space=pl.ANY)],
        out_specs=whole(shape),
        out_shape=jax.ShapeDtypeStruct(shape, BF),
        cost_estimate=cost(0, 4 * shape[0] * shape[1]),
        compiler_params=params(12),
    )(*parts, after)


def cost(flops, size):
    return pl.CostEstimate(flops=flops, bytes_accessed=size, transcendentals=0)


def over_x(value, partner):
    return lax.ppermute(value, "grp", [(source, source ^ partner) for source in range(GROUPS)])


def gather_over_x(value):
    return [value] + [over_x(value, partner) for partner in range(1, PARTNERS + 1)]


def product(left, right):
    return lax.dot_general(left, right, NT, preferred_element_type=F32)


def on_device(
    queries, key_rows, value_rows, output_rows, output_grad, log_normalizer, selection,
    query_weight, key_weight, value_weight,
):
    smem = pl.BlockSpec(memory_space=pltpu.SMEM)
    whole = lambda shape: pl.BlockSpec(shape, lambda step: (0,) * len(shape))
    hbm = pl.BlockSpec(memory_space=pl.ANY)
    index = lax.axis_index("ctx").astype(jnp.int32)
    place = index.reshape(1)
    group = jnp.stack([lax.axis_index("grp").astype(jnp.int32), index % 2])
    count = lax.axis_size("ctx")
    norm = log_normalizer.T.reshape(HEADS, 1, BLOCK)
    rows, pieces_shape = (BLOCK, 2 * HD), (BLOCKS, SLOTS, PIECE, 2 * HD)
    tile_flops = 10 * HEADS * HD * BLOCK * BLOCK

    own = pl.pallas_call(
        join_kernel,
        grid=(1,),
        in_specs=[whole(key_rows.shape), whole(value_rows.shape)],
        out_specs=whole(rows),
        out_shape=jax.ShapeDtypeStruct(rows, BF),
        cost_estimate=cost(0, 8 * BLOCK * HD),
        compiler_params=PARAMS,
    )(key_rows, value_rows)
    weights = (query_weight, key_weight, value_weight)
    *packed, pack_done = pack_weights(group, weights)
    direct = [over_x(part, index + 1) for index, part in enumerate(packed)]
    before = lax.ppermute(own, "ctx", [(i, (i + 1) % count) for i in range(count)])
    pieces = lax.all_to_all(own.reshape(BLOCKS, PIECE, 2 * HD), "ctx", 0, 0)
    picked = pl.pallas_call(
        pick_kernel,
        grid=(1,),
        in_specs=[smem, whole(pieces.shape)],
        out_specs=whole(pieces_shape),
        out_shape=jax.ShapeDtypeStruct(pieces_shape, BF),
        cost_estimate=cost(0, 12 * BLOCK * HD),
        compiler_params=params(8),
    )(selection, pieces)
    chosen = lax.all_to_all(picked, "ctx", 0, 0)

    near_in = (queries, output_grad, output_rows, norm, own, before)
    delta, query_near, own_grad, before_grad = pl.pallas_call(
        near_kernel,
        grid=(1,),
        in_specs=[smem] + [whole(array.shape) for array in near_in],
        out_specs=[whole((HEADS, 1, BLOCK)), whole((HEADS, HD, BLOCK)), whole(rows), whole(rows)],
        out_shape=[
            jax.ShapeDtypeStruct((HEADS, 1, BLOCK), F32),
            jax.ShapeDtypeStruct((HEADS, HD, BLOCK), F32),
            jax.ShapeDtypeStruct(rows, F32),
            jax.ShapeDtypeStruct(rows, BF),
        ],
        scratch_shapes=tile_scratch(0),
        cost_estimate=cost(600 * tile_flops, 1 << 22),
        compiler_params=PARAMS,
    )(place, *near_in)
    before_sum = lax.ppermute(before_grad, "ctx", [(i, (i - 1) % count) for i in range(count)])

    far_in = (queries, output_grad, norm, delta, query_near, chosen)
    query_grad, chosen_grad, far_done = pl.pallas_call(
        far_kernel,
        grid=(1,),
        in_specs=[smem, smem] + [whole(array.shape) for array in far_in],
        out_specs=[whole((BLOCK, HEADS * HD)), whole(pieces_shape), whole(TOKEN)],
        out_shape=[
            jax.ShapeDtypeStruct((BLOCK, HEADS * HD), BF),
            jax.ShapeDtypeStruct(pieces_shape, BF),
            jax.ShapeDtypeStruct(TOKEN, BF),
        ],
        scratch_shapes=tile_scratch(1),
        cost_estimate=cost(6 * tile_flops, 1 << 22),
        compiler_params=PARAMS,
    )(place, selection, *far_in)

    returned = lax.all_to_all(chosen_grad, "ctx", 0, 0)
    *direct, far_done = lax.optimization_barrier((*direct, far_done))
    swapped = [lax.ppermute(part, "ctx", [(i, i ^ 1) for i in range(count)]) for part in direct]
    query_all_weight, near_kept, near_sent, done = unpack_weights(group, weights, direct, swapped, far_done)
    query_parts = gather_over_x(query_grad)
    collected = pl.pallas_call(
        collect_kernel,
        grid=(1,),
        in_specs=[smem, whole(pieces_shape)],
        out_specs=whole(pieces.shape),
        out_shape=jax.ShapeDtypeStruct((BLOCKS, PIECE, 2 * HD), BF),
        scratch_shapes=[pltpu.VMEM((BLOCKS, PIECE, 2 * HD), F32)],
        cost_estimate=cost(0, 12 * BLOCK * HD),
        compiler_params=params(8),
    )(selection, returned)
    part = product(join_queries(query_parts, collected), query_all_weight)
    kept_part, sent_part = part[:, :BLOCK], part[:, BLOCK:]
    chosen_sum = lax.all_to_all(collected, "ctx", 0, 0).reshape(rows)
    chosen_sum, kept_part, sent_part = lax.optimization_barrier((chosen_sum, kept_part, sent_part))
    factor = jnp.where(lax.broadcasted_iota(jnp.int32, rows, 1) < HD, SCALE, 1.0)
    near_grad = ((own_grad + before_sum.astype(F32) + chosen_sum.astype(F32)) * factor).astype(BF)
    half = BLOCK // HALVES
    pairs = [(source, source ^ OTHER) for source in range(GROUPS)]
    near_parts = [gather_over_x(near_grad[i * half : (i + 1) * half]) for i in range(HALVES)]
    kept, got = [], []
    for i, near_all in enumerate(near_parts):
        some = slice(i * half, (i + 1) * half)
        near_all = jnp.concatenate(near_all, axis=1)
        sent = (sent_part[some] + product(near_all, near_sent)).astype(BF)
        got.append(lax.ppermute(sent, "grp", pairs))
        kept.append(kept_part[some] + product(near_all, near_kept))
    kept = lax.optimization_barrier(kept)
    return jnp.concatenate([(part + other.astype(F32)).astype(BF) for part, other in zip(kept, got)], axis=0)


def solution(mesh):
    tokens = P("ctx", "grp")
    return jax.shard_map(
        on_device,
        mesh=mesh,
        in_specs=(tokens,) * 6 + (P(),) + (P(None, "grp"),) * 3,
        out_specs=tokens,
        check_vma=False,
    )
```

```python
import jax
import jax.numpy as jnp
from jax import lax
from jax.experimental import pallas as pl
from jax.experimental.pallas import tpu as pltpu
from jax.sharding import PartitionSpec as P

HD = 128
HEADS = 4
BLOCK = 512
BLOCKS = 32
PIECE = BLOCK // BLOCKS
SLOTS = 2
GROUPS = 8
SCALE = float(HD) ** (-0.5)
LOG2E = 1.4426950408889634
BF = jnp.bfloat16
F32 = jnp.float32
VMEM_BYTES = 60 * 1024 * 1024
PARAMS = pltpu.CompilerParams(vmem_limit_bytes=VMEM_BYTES)


def params(mib):
    return pltpu.CompilerParams(vmem_limit_bytes=mib * 1024 * 1024)


PARTNERS = 3
HALVES = 2
TOKEN = (16, HD)
OTHER = 4

NT = (((1,), (1,)), ((), ()))


def others(selection, block):
    before = block - 1
    first, second, third = selection[block, 0], selection[block, 1], selection[block, 2]
    return jnp.where(first == before, second, first), jnp.where(third == before, second, third)


def pick_kernel(selection, pieces, *refs):
    out = refs[-1]

    def step(block, carry):
        for slot, chosen in enumerate(others(selection, block)):
            out[block, slot] = pieces[chosen]
        return carry

    lax.fori_loop(0, BLOCKS, step, 0, unroll=True)


def collect_kernel(selection, parts, *refs):
    out, total = refs[-2:]
    total[...] = jnp.zeros_like(total)

    def step(block, carry):
        for slot, chosen in enumerate(others(selection, block)):
            total[chosen] += jnp.where(chosen < block, parts[block, slot].astype(F32), 0.0)

        return carry

    lax.fori_loop(0, BLOCKS, step, 0, unroll=True)
    out[...] = total[...].astype(BF)


def attend(queries, output_grad, norm, delta, scratch, causal):
    keys, values, keys_t, query_total, key_total, value_total = scratch
    key_total[...] = jnp.zeros_like(key_total)
    value_total[...] = jnp.zeros_like(value_total)
    key, value, key_t = keys[...], values[...], keys_t[...]

    def head_step(head, carry):
        cols = pl.ds(pl.multiple_of(head * HD, HD), HD)
        query, grad = queries[:, cols], output_grad[:, cols]
        scores = lax.dot_general(key, query, NT, preferred_element_type=F32)
        prob_grad = lax.dot_general(value, grad, NT, preferred_element_type=F32)
        probs = jnp.exp2(scores * (SCALE * LOG2E) - norm[head] * LOG2E)
        if causal:
            shape = (BLOCK, BLOCK)
            seen = lax.broadcasted_iota(jnp.int32, shape, 0) <= lax.broadcasted_iota(jnp.int32, shape, 1)
            probs = jnp.where(seen, probs, 0.0)
        score_half = (probs * (prob_grad - delta[head])).astype(BF)
        value_total[...] += jnp.dot(probs.astype(BF), grad, preferred_element_type=F32)
        key_total[...] += jnp.dot(score_half, query, preferred_element_type=F32)
        query_total[head] += jnp.dot(key_t, score_half, preferred_element_type=F32)
        return carry

    lax.fori_loop(0, HEADS, head_step, 0, unroll=True)


def load(scratch, key, value):
    keys, values, keys_t = scratch[:3]
    keys[...] = key
    values[...] = value
    keys_t[...] = key.astype(F32).T.astype(BF)


def near_kernel(
    place, queries, output_grad, output_rows, norm, own, before,
    delta, query_total, own_out, before_out, keys, values, keys_t, key_total, value_total,
):
    scratch = (keys, values, keys_t, query_total, key_total, value_total)
    for head in range(HEADS):
        cols = pl.ds(head * HD, HD)
        product = output_rows[:, cols].astype(F32) * output_grad[:, cols].astype(F32)
        delta[head] = jnp.sum(product.T, axis=0, keepdims=True)
    query_total[...] = jnp.zeros_like(query_total)
    load(scratch, own[:, :HD], own[:, HD:])
    attend(queries, output_grad, norm, delta, scratch, True)
    own_out[:, :HD] = key_total[...]
    own_out[:, HD:] = value_total[...]

    @pl.when(place[0] > 0)
    def _():
        load(scratch, before[:, :HD], before[:, HD:])
        attend(queries, output_grad, norm, delta, scratch, False)
        before_out[:, :HD] = key_total[...].astype(BF)
        before_out[:, HD:] = value_total[...].astype(BF)

    @pl.when(place[0] == 0)
    def _():
        before_out[...] = jnp.zeros_like(before_out)


def far_kernel(
    place, selection, queries, output_grad, norm, delta, query_near, chosen,
    query_out, chosen_out, done, keys, values, keys_t, query_total, key_total, value_total,
):
    done[...] = jnp.zeros_like(done)
    scratch = (keys, values, keys_t, query_total, key_total, value_total)
    block = place[0]
    query_total[...] = query_near[...]
    for slot, pick in enumerate(others(selection, block)):

        @pl.when(pick < block)
        def _():
            load(
                scratch,
                chosen[:, slot, :, :HD].reshape(BLOCK, HD),
                chosen[:, slot, :, HD:].reshape(BLOCK, HD),
            )
            attend(queries, output_grad, norm, delta, scratch, False)
            chosen_out[:, slot, :, :HD] = key_total[...].reshape(BLOCKS, PIECE, HD).astype(BF)
            chosen_out[:, slot, :, HD:] = value_total[...].reshape(BLOCKS, PIECE, HD).astype(BF)

        @pl.when(pick >= block)
        def _():
            chosen_out[:, slot] = jnp.zeros((BLOCKS, PIECE, 2 * HD), BF)

    for head in range(HEADS):
        query_out[:, head * HD : (head + 1) * HD] = (query_total[head].T * SCALE).astype(BF)


def tile_scratch(with_query):
    shapes = [((BLOCK, HD), BF), ((BLOCK, HD), BF), ((HD, BLOCK), BF)]
    shapes += [((HEADS, HD, BLOCK), F32)] * with_query + [((BLOCK, HD), F32)] * 2
    return [pltpu.VMEM(shape, dtype) for shape, dtype in shapes]


def join_kernel(key_rows, value_rows, out):
    out[:, :HD] = key_rows[...]
    out[:, HD:] = value_rows[...]


def pack_kernel(place, *refs):
    wide = HEADS * HD
    done = refs[-1]
    done[...] = jnp.zeros_like(done)
    for partner in range(PARTNERS):
        query, key, value = refs[3 * partner : 3 * partner + 3]
        out = refs[3 * PARTNERS + partner]
        out[:, :wide] = query[...]
        out[:, wide : wide + HD] = key[...]
        out[:, wide + HD :] = value[...]


def pack_weights(place, weights):
    steps = 1
    rows, width = BLOCK // steps, (HEADS + 2) * HD

    def index(partner):
        return lambda step, place: ((place[0] ^ (place[1] * OTHER) ^ partner) * steps + step, 0)

    partners = range(1, PARTNERS + 1)
    return pl.pallas_call(
        pack_kernel,
        grid_spec=pltpu.PrefetchScalarGridSpec(
            num_scalar_prefetch=1,
            grid=(steps,),
            in_specs=[
                pl.BlockSpec((rows, weight.shape[1]), index(partner)) for partner in partners for weight in weights
            ],
            out_specs=[pl.BlockSpec((rows, width), lambda step, place: (step, 0))] * PARTNERS
            + [pl.BlockSpec(TOKEN, lambda step, place: (0, 0))],
        ),
        out_shape=[jax.ShapeDtypeStruct((BLOCK, width), BF)] * PARTNERS + [jax.ShapeDtypeStruct(TOKEN, BF)],
        cost_estimate=cost(0, 4 * PARTNERS * BLOCK * width),
        compiler_params=PARAMS,
    )(place, *weights * PARTNERS)


def unpack_kernel(place, *refs):
    direct, swapped, refs = refs[:PARTNERS], refs[PARTNERS : 2 * PARTNERS], refs[2 * PARTNERS :]
    own, (query_out, kept, sent, done) = (refs[:3], refs[3:6]), refs[7:]
    done[...] = jnp.zeros_like(done)
    wide = HEADS * HD

    def run(first, second):
        for side, (out, parts) in enumerate(((kept, first), (sent, second))):
            rows = slice(side * BLOCK, (side + 1) * BLOCK)
            query, key, value = own[side]
            query_out[rows, :wide] = query[...]
            out[:, :HD] = key[...]
            out[:, HD : 2 * HD] = value[...]
            for index, part in enumerate(parts):
                query_out[rows, (index + 1) * wide : (index + 2) * wide] = part[:, :wide]
                out[:, (index + 1) * 2 * HD : (index + 2) * 2 * HD] = part[:, wide:]

    @pl.when(place[1] == 0)
    def _():
        run(direct, swapped)

    @pl.when(place[1] == 1)
    def _():
        run(swapped, direct)


def unpack_weights(place, weights, direct, swapped, after):
    part = pl.BlockSpec((BLOCK, (HEADS + 2) * HD), lambda step, place: (0, 0))
    kept = [pl.BlockSpec((BLOCK, weight.shape[1]), lambda step, place: (place[0], 0)) for weight in weights]
    sent = [pl.BlockSpec((BLOCK, weight.shape[1]), lambda step, place: (place[0] ^ OTHER, 0)) for weight in weights]
    near = (BLOCK, (PARTNERS + 1) * 2 * HD)
    shapes = [(2 * BLOCK, (PARTNERS + 1) * HEADS * HD), near, near, TOKEN]
    return pl.pallas_call(
        unpack_kernel,
        grid_spec=pltpu.PrefetchScalarGridSpec(
            num_scalar_prefetch=1,
            grid=(1,),
            in_specs=[part] * (2 * PARTNERS) + kept + sent + [pl.BlockSpec(memory_space=pl.ANY)],
            out_specs=[pl.BlockSpec(shape, lambda step, place: (0, 0)) for shape in shapes],
        ),
        out_shape=[jax.ShapeDtypeStruct(shape, BF) for shape in shapes],
        cost_estimate=cost(0, 4 * sum(rows * cols for rows, cols in shapes)),
        compiler_params=PARAMS,
    )(place, *direct, *swapped, *weights, *weights, after)


def join_queries_kernel(*refs):
    out = refs[-1]
    for index, part in enumerate(refs[: PARTNERS + 1]):
        out[:, index * HEADS * HD : (index + 1) * HEADS * HD] = part[...]


def join_queries(parts, after):
    shape = (BLOCK, (PARTNERS + 1) * HEADS * HD)
    whole = lambda shape: pl.BlockSpec(shape, lambda step: (0, 0))
    return pl.pallas_call(
        join_queries_kernel,
        grid=(1,),
        in_specs=[whole(part.shape) for part in parts] + [pl.BlockSpec(memory_space=pl.ANY)],
        out_specs=whole(shape),
        out_shape=jax.ShapeDtypeStruct(shape, BF),
        cost_estimate=cost(0, 4 * shape[0] * shape[1]),
        compiler_params=params(12),
    )(*parts, after)


def cost(flops, size):
    return pl.CostEstimate(flops=flops, bytes_accessed=size, transcendentals=0)


def over_x(value, partner):
    return lax.ppermute(value, "grp", [(source, source ^ partner) for source in range(GROUPS)])


def gather_over_x(value):
    return [value] + [over_x(value, partner) for partner in range(1, PARTNERS + 1)]


def product(left, right):
    return lax.dot_general(left, right, NT, preferred_element_type=F32)


def on_device(
    queries, key_rows, value_rows, output_rows, output_grad, log_normalizer, selection,
    query_weight, key_weight, value_weight,
):
    smem = pl.BlockSpec(memory_space=pltpu.SMEM)
    whole = lambda shape: pl.BlockSpec(shape, lambda step: (0,) * len(shape))
    hbm = pl.BlockSpec(memory_space=pl.ANY)
    index = lax.axis_index("ctx").astype(jnp.int32)
    place = index.reshape(1)
    group = jnp.stack([lax.axis_index("grp").astype(jnp.int32), index % 2])
    count = lax.axis_size("ctx")
    norm = log_normalizer.T.reshape(HEADS, 1, BLOCK)
    rows, pieces_shape = (BLOCK, 2 * HD), (BLOCKS, SLOTS, PIECE, 2 * HD)
    tile_flops = 10 * HEADS * HD * BLOCK * BLOCK

    own = pl.pallas_call(
        join_kernel,
        grid=(1,),
        in_specs=[whole(key_rows.shape), whole(value_rows.shape)],
        out_specs=whole(rows),
        out_shape=jax.ShapeDtypeStruct(rows, BF),
        cost_estimate=cost(0, 8 * BLOCK * HD),
        compiler_params=PARAMS,
    )(key_rows, value_rows)
    weights = (query_weight, key_weight, value_weight)
    *packed, pack_done = pack_weights(group, weights)
    direct = [over_x(part, index + 1) for index, part in enumerate(packed)]
    before = lax.ppermute(own, "ctx", [(i, (i + 1) % count) for i in range(count)])
    pieces = lax.all_to_all(own.reshape(BLOCKS, PIECE, 2 * HD), "ctx", 0, 0)
    picked = pl.pallas_call(
        pick_kernel,
        grid=(1,),
        in_specs=[smem, whole(pieces.shape)],
        out_specs=whole(pieces_shape),
        out_shape=jax.ShapeDtypeStruct(pieces_shape, BF),
        cost_estimate=cost(0, 12 * BLOCK * HD),
        compiler_params=params(8),
    )(selection, pieces)
    chosen = lax.all_to_all(picked, "ctx", 0, 0)

    near_in = (queries, output_grad, output_rows, norm, own, before)
    delta, query_near, own_grad, before_grad = pl.pallas_call(
        near_kernel,
        grid=(1,),
        in_specs=[smem] + [whole(array.shape) for array in near_in],
        out_specs=[whole((HEADS, 1, BLOCK)), whole((HEADS, HD, BLOCK)), whole(rows), whole(rows)],
        out_shape=[
            jax.ShapeDtypeStruct((HEADS, 1, BLOCK), F32),
            jax.ShapeDtypeStruct((HEADS, HD, BLOCK), F32),
            jax.ShapeDtypeStruct(rows, F32),
            jax.ShapeDtypeStruct(rows, BF),
        ],
        scratch_shapes=tile_scratch(0),
        cost_estimate=cost(600 * tile_flops, 1 << 22),
        compiler_params=PARAMS,
    )(place, *near_in)
    before_sum = lax.ppermute(before_grad, "ctx", [(i, (i - 1) % count) for i in range(count)])

    far_in = (queries, output_grad, norm, delta, query_near, chosen)
    query_grad, chosen_grad, far_done = pl.pallas_call(
        far_kernel,
        grid=(1,),
        in_specs=[smem, smem] + [whole(array.shape) for array in far_in],
        out_specs=[whole((BLOCK, HEADS * HD)), whole(pieces_shape), whole(TOKEN)],
        out_shape=[
            jax.ShapeDtypeStruct((BLOCK, HEADS * HD), BF),
            jax.ShapeDtypeStruct(pieces_shape, BF),
            jax.ShapeDtypeStruct(TOKEN, BF),
        ],
        scratch_shapes=tile_scratch(1),
        cost_estimate=cost(6 * tile_flops, 1 << 22),
        compiler_params=PARAMS,
    )(place, selection, *far_in)

    returned = lax.all_to_all(chosen_grad, "ctx", 0, 0)
    *direct, far_done = lax.optimization_barrier((*direct, far_done))
    swapped = [lax.ppermute(part, "ctx", [(i, i ^ 1) for i in range(count)]) for part in direct]
    query_all_weight, near_kept, near_sent, done = unpack_weights(group, weights, direct, swapped, far_done)
    query_parts = gather_over_x(query_grad)
    collected = pl.pallas_call(
        collect_kernel,
        grid=(1,),
        in_specs=[smem, whole(pieces_shape)],
        out_specs=whole(pieces.shape),
        out_shape=jax.ShapeDtypeStruct((BLOCKS, PIECE, 2 * HD), BF),
        scratch_shapes=[pltpu.VMEM((BLOCKS, PIECE, 2 * HD), F32)],
        cost_estimate=cost(0, 12 * BLOCK * HD),
        compiler_params=params(8),
    )(selection, returned)
    part = product(join_queries(query_parts, collected), query_all_weight)
    kept_part, sent_part = part[:, :BLOCK], part[:, BLOCK:]
    chosen_sum = lax.all_to_all(collected, "ctx", 0, 0).reshape(rows)
    chosen_sum, kept_part, sent_part = lax.optimization_barrier((chosen_sum, kept_part, sent_part))
    factor = jnp.where(lax.broadcasted_iota(jnp.int32, rows, 1) < HD, SCALE, 1.0)
    near_grad = ((own_grad + before_sum.astype(F32) + chosen_sum.astype(F32)) * factor).astype(BF)
    half = BLOCK // HALVES
    pairs = [(source, source ^ OTHER) for source in range(GROUPS)]
    near_parts = [gather_over_x(near_grad[i * half : (i + 1) * half]) for i in range(HALVES)]
    kept, got = [], []
    for i, near_all in enumerate(near_parts):
        some = slice(i * half, (i + 1) * half)
        near_all = jnp.concatenate(near_all, axis=1)
        sent = (sent_part[some] + product(near_all, near_sent)).astype(BF)
        got.append(lax.ppermute(sent, "grp", pairs))
        kept.append(kept_part[some] + product(near_all, near_kept))
    kept = lax.optimization_barrier(kept)
    return jnp.concatenate([(part + other.astype(F32)).astype(BF) for part, other in zip(kept, got)], axis=0)


def solution(mesh):
    tokens = P("ctx", "grp")
    return jax.shard_map(
        on_device,
        mesh=mesh,
        in_specs=(tokens,) * 6 + (P(),) + (P(None, "grp"),) * 3,
        out_specs=tokens,
        check_vma=False,
    )
```
